128 devices in a mesh: band: 16 (over x, y_hi, core), grid: 8 (over z, y_lo).
Axes of the slice: x: 4, y: 4 (y_hi: 2, y_lo: 2; y = y_hi * 2 + y_lo), z: 4, core: 2. Of those that a mesh axis runs over, the one named last changes fastest.
Arguments:
- orbitals: float32 [64, 64, 4096], P('band', 'grid'), may hold values from -6 to 6
- kernel: float32 [64, 64, 64], P(None, 'grid'), may hold values from 0.05 to 18, as said below
Outputs:
- applied: float32 [64, 64, 4096], P('band', 'grid')
The draws below stay inside these ranges and needn't reach their ends.
Inputs may be any that keep to these rules, and one draw needn't show every extreme that they name: The kernel is even and positive: kernel[kx, ky, kz] equals kernel[(-kx) mod 64, (-ky) mod 64, (-kz) mod 64].
All inputs are finite; a program needn't handle non-finite values.
Results may differ from the reference program's by a relative error of at most 0.0003.
Values sent between devices are 32-bit elements; how exact they have to be, the bound alone decides.
A program may use at most 192 MiB of HBM per device.

```python
import math
import jax
import jax.numpy as jnp
from jax import lax

GRID = 64
BAND_DEV = 4
STOPS = 3
BANDS = 64
N_BAND = 16


def draw_kernel(key, part):
    key = jax.random.fold_in(key, 7)
    random_part = jnp.exp(jax.random.uniform(key, (GRID, GRID, GRID), jnp.float32, math.log(0.1), math.log(4.0)))
    mirrored = jnp.roll(jnp.flip(random_part, (0, 1, 2)), 1, (0, 1, 2))
    values = 0.5 * (random_part + mirrored)
    return values


def block_scale(rng, shape, cuts, smallest, top_value):
    level = 1.0
    for position, shards_of in cuts:
        heights = jax.random.uniform(jax.random.fold_in(jax.random.fold_in(rng, 6), position), (shards_of,), jnp.float32, smallest / len(cuts), top_value / len(cuts))
        level = level * jnp.repeat(jnp.exp(heights), shape[position] // shards_of).reshape((-1,) + (1,) * (len(shape) - 1 - position))
    return level


def normal_values(stream_key, dims, width, limit, split=(), kind=jnp.bfloat16):
    values = jax.random.normal(stream_key, dims, jnp.float32) * width
    if len(split) > 0:
        values = block_scale(stream_key, dims, split, -0.22, 0.18) * values
    return jnp.clip(values, min=-limit, max=limit).astype(kind)


def setup_inputs(seed: int = 0) -> dict:
    key_list = jax.random.split(jax.random.key(seed), 3)
    orbitals = normal_values(key_list[0], (BANDS, GRID, GRID * GRID), 1.0, 6.0, ((0, 16), (1, 8)), jnp.float32)
    kernel = draw_kernel(jax.random.fold_in(key_list[2], 71), 0)
    return dict(orbitals=orbitals, kernel=kernel)


def reference(orbitals, kernel):
    extent = GRID
    groups = orbitals.reshape(N_BAND, BAND_DEV, extent, extent, extent)
    half_kernel = kernel[:, :, : extent // 2 + 1]

    def one_group(group_index):
        targets = lax.dynamic_index_in_dim(groups, group_index, 0, keepdims=False)
        accumulated = jnp.zeros(targets.shape, jnp.float32)
        for stop_index in range(STOPS):
            source = ((group_index - stop_index) % N_BAND).astype(jnp.int32)
            partners = lax.dynamic_index_in_dim(groups, source, 0, keepdims=False)
            densities = targets[:, None] * partners[None]
            spectrum = jnp.fft.rfftn(densities, axes=(2, 3, 4))
            potentials = jnp.fft.irfftn(spectrum * half_kernel, s=(extent, extent, extent), axes=(2, 3, 4))
            accumulated = accumulated + jnp.sum(potentials * partners[None], axis=1)
        return -accumulated

    applied = lax.map(one_group, jnp.arange(N_BAND, dtype=jnp.int32))
    return applied.reshape(BAND_DEV * N_BAND, extent, extent * extent)
```

```python
import functools
import math

import jax
import jax.numpy as jnp
import ml_dtypes
import numpy as np
from jax import lax
from jax.experimental import pallas as pl
from jax.experimental.pallas import tpu as pltpu
from jax.sharding import PartitionSpec as P

G = 64
BF = jnp.bfloat16
F32 = jnp.float32
H = math.sqrt(0.5)
MESH = pl.DeviceIdType.MESH
YA = 4
KC = 8


def split_table(matrix):
    hi = matrix.astype(ml_dtypes.bfloat16)
    return hi, (matrix - hi.astype(np.float64)).astype(ml_dtypes.bfloat16)


def tables():
    k = np.arange(G)
    angle = 2.0 * np.pi * ((k[:, None] * k[None, :]) % G) / G
    c, s = np.cos(angle), np.sin(angle)

    def left(matrix):
        hi, lo = split_table(matrix)
        return np.concatenate([hi, hi, lo], 1)

    def right(matrix):
        hi, lo = split_table(matrix)
        return np.concatenate([hi, hi, lo], 0)

    forward_x = left(np.block([[c, s], [-s, c]]))
    inverse_x = left(np.block([[c, -s], [s, c]]))
    parity = np.array([[1.0, 1.0], [1.0, -1.0]])
    cc, ss = np.kron(parity, c), np.kron(parity, s)
    forward_z = right(np.block([[cc, -ss], [ss, cc]]))
    inverse_z = right(np.block([[cc, ss], [-ss, cc]]) * (-1.0 / G**3))
    twiddle = np.ones((32, 2, 8, 128), np.float64)
    turn = 2.0 * np.pi * np.arange(32) / G
    twiddle[:, 0, :, 64:] = np.cos(turn)[:, None, None]
    twiddle[:, 1, :, :64] = 0.0
    twiddle[:, 1, :, 64:] = np.sin(turn)[:, None, None]
    return forward_x, inverse_x, forward_z, inverse_z, twiddle.astype(np.float32)


def cadd(a, b):
    return a[0] + b[0], a[1] + b[1]


def csub(a, b):
    return a[0] - b[0], a[1] - b[1]


def rot(a, sign):
    return (-a[1], a[0]) if sign > 0 else (a[1], -a[0])


def dft4(v, sign):
    p, q = cadd(v[0], v[2]), csub(v[0], v[2])
    r, t = cadd(v[1], v[3]), csub(v[1], v[3])
    t = rot(t, sign)
    return [cadd(p, r), cadd(q, t), csub(p, r), csub(q, t)]


def dft8(v, sign):
    e = dft4(v[0::2], sign)
    o = dft4(v[1::2], sign)
    a, b = o[1], o[3]
    if sign > 0:
        o[1] = (H * (a[0] - a[1]), H * (a[0] + a[1]))
        o[3] = (-H * (b[0] + b[1]), H * (b[0] - b[1]))
    else:
        o[1] = (H * (a[0] + a[1]), H * (a[1] - a[0]))
        o[3] = (H * (b[1] - b[0]), -H * (b[0] + b[1]))
    o[2] = rot(o[2], sign)
    return [cadd(e[i], o[i]) for i in range(4)] + [csub(e[i], o[i]) for i in range(4)]


def dft32(load, store, sign):
    mid = {}
    for n2 in range(4):
        out = dft8([load(4 * n1 + n2) for n1 in range(8)], sign)
        for k1 in range(8):
            v = out[k1]
            if n2 * k1 == 4:
                v = (H * (v[0] - sign * v[1]), H * (v[1] + sign * v[0]))
            elif n2 * k1:
                turn = sign * 2.0 * math.pi * n2 * k1 / 32
                c, s = math.cos(turn), math.sin(turn)
                v = (v[0] * c - v[1] * s, v[0] * s + v[1] * c)
            mid[n2, k1] = v
    for k1 in range(8):
        out = dft4([mid[n2, k1] for n2 in range(4)], sign)
        for k2 in range(4):
            store(k1 + 8 * k2, out[k2])


def split(x):
    hi = x.astype(BF)
    return hi, (x - hi.astype(F32)).astype(BF)


def dot(a, b):
    return jnp.dot(a, b, preferred_element_type=F32)


def columns(base, count=1):
    return pl.ds(pl.multiple_of(base * 128, 128), count * 128)


def forward_columns(t, phi, fx, z):
    @pl.loop(0, 32 // YA)
    def _(step):
        at = columns(step * YA, YA)
        tv = t[:, :, at].reshape(G, YA * 128)
        pairs = [tv * phi[k, :, :, at].reshape(G, YA * 128) for k in range(2)]
        hi, lo = split(jnp.concatenate(pairs, 0))
        res = dot(fx[...], jnp.concatenate([hi, lo, hi], 0))
        for i in range(YA):
            z[step * YA + i] = res[:, 128 * i : 128 * (i + 1)]


def forward_rows(tw, z):
    @pl.loop(0, 8)
    def _(tile):
        rr = pl.ds(pl.multiple_of(tile * 8, 8), 8)
        ri = pl.ds(pl.multiple_of(64 + tile * 8, 8), 8)

        def load(n):
            return z[n, rr, :], z[n, ri, :]

        def store(k, v):
            c, s = tw[k, 0], tw[k, 1]
            z[k, rr, :] = v[0] * c + v[1] * s
            z[k, ri, :] = v[1] * c - v[0] * s

        dft32(load, store, -1)


def middle(kern, fz, iz, z):
    @pl.loop(0, 32 // KC)
    def _(step):
        ks = pl.ds(step * KC, KC)
        a = jnp.concatenate([z[ks, 0:64, :].reshape(KC * 64, 128), z[ks, 64:128, :].reshape(KC * 64, 128)], 1)
        hi, lo = split(a)
        b = dot(jnp.concatenate([hi, lo, hi], 1), fz[...])
        kv = kern[ks].reshape(KC * 64, 128)
        hi, lo = split(b * jnp.concatenate([kv, kv], 1))
        b = dot(jnp.concatenate([hi, lo, hi], 1), iz[...])
        z[ks, 0:64, :] = b[:, :128].reshape(KC, 64, 128)
        z[ks, 64:128, :] = b[:, 128:].reshape(KC, 64, 128)


def inverse_rows(tw, z):
    @pl.loop(0, 8)
    def _(tile):
        rr = pl.ds(pl.multiple_of(tile * 8, 8), 8)
        ri = pl.ds(pl.multiple_of(64 + tile * 8, 8), 8)

        def load(n):
            c, s = tw[n, 0], tw[n, 1]
            r, i = z[n, rr, :], z[n, ri, :]
            return r * c - i * s, i * c + r * s

        def store(k, v):
            z[k, rr, :] = v[0]
            z[k, ri, :] = v[1]

        dft32(load, store, 1)


def inverse_columns(phi, ix, z, part):
    @pl.loop(0, 32 // YA)
    def _(step):
        at = columns(step * YA, YA)
        hi, lo = split(jnp.concatenate([z[step * YA + i] for i in range(YA)], 1))
        res = dot(ix[...], jnp.concatenate([hi, lo, hi], 0))
        v = res[:64] * phi[0, :, :, at].reshape(G, YA * 128) + res[64:] * phi[1, :, :, at].reshape(G, YA * 128)
        v = v.reshape(4, 2, 8, YA * 128)
        part[0, :, :, at] = v[:, 0]
        part[1, :, :, at] = v[:, 1]


def unpack_kernel(kp, kern):
    low = lax.broadcasted_iota(jnp.int32, (64, 128), 1) < 64

    @pl.loop(0, 4)
    def _(slab):
        @pl.loop(0, 4)
        def _(r):
            a, b = kp[slab, r], kp[slab + 4, r]
            kern[slab * 8 + r] = jnp.where(low, a, pltpu.roll(b, 64, 1))
            kern[slab * 8 + 4 + r] = jnp.where(low, pltpu.roll(a, 64, 1), b)


def body(orb, kpk, fx, ix, fz, iz, tw, out, phi, targ, kp, kern, z, part, rcore, rhalo, total, send, recv, local):
    b = lax.axis_index("band")
    q = lax.axis_index("grid")
    core, block, x = b % 2, b // 2, b // 4
    plane, ylo = q // 2, q % 2
    chip = block * 2 + ylo
    sibling = (block * 2 + 1 - core, q)

    def device(h, c, zz):
        h = (h + 16) % 16
        return ((h // 2) * 2 + c, zz * 2 + h % 2)

    def remote(src, dst, s, r, where):
        return pltpu.make_async_remote_copy(
            src_ref=src, dst_ref=dst, send_sem=send.at[s], recv_sem=recv.at[r], device_id=where, device_id_type=MESH
        )

    barrier = pltpu.get_barrier_semaphore()
    greeted = []
    for dc in range(2):
        for dq in range(8):
            if dc or dq:
                greeted.append(((b + dc) % 2 + block * 2, (q + dq) % 8))
    for dh in (-2, -1, 1, 2, 4, 8, 12):
        greeted.append(device(chip + dh, core, plane))
    for where in greeted:
        pl.semaphore_signal(barrier, inc=1, device_id=where, device_id_type=MESH)
    pl.semaphore_wait(barrier, len(greeted))

    def slab(s):
        return pl.ds(s, 1)

    def first(c):
        src = orb.at[pl.ds(2 * c, 2)].reshape(2, 1, 8, 4096)
        return src, phi.at[:, slab(q)]

    mine = core == ylo
    for dc in range(2):
        c = (core + dc) % 2
        src, dst = first(c)
        cp = remote(src, dst, dc, ylo, (block * 2 + c, plane * 2 + core))
        if dc == 0:
            keep = pltpu.make_async_copy(src, dst, local.at[0])

            @pl.when(mine)
            def _():
                keep.start()

            @pl.when(jnp.logical_not(mine))
            def _():
                cp.start()

            keep_remote = cp
        else:
            cp.start()
            first_send = cp

    kx_half = pl.ds(pl.multiple_of(32 * core, 32), 32)
    kernel_keep = pltpu.make_async_copy(kpk.at[x, kx_half], kp.at[q, x, kx_half], local.at[1])
    kernel_keep.start()
    kernel_first = [
        remote(kpk.at[x, kx_half], kp.at[q, x, kx_half], 1 + d, 1 + d, (b, (q + d) % 8)) for d in range(1, 8)
    ]
    for cp in kernel_first:
        cp.start()

    spread = []
    for i in range(2):
        p = (ylo + i) % 2
        s = 2 * plane + p
        if i == 0:

            @pl.when(mine)
            def _():
                keep.wait()

            @pl.when(jnp.logical_not(mine))
            def _():
                remote(phi.at[:, slab(s)], phi.at[:, slab(s)], 0, p, (b, q)).wait_recv()
        else:
            remote(phi.at[:, slab(s)], phi.at[:, slab(s)], 0, p, (b, q)).wait_recv()
        for d in (1, 3, 2):
            cp = remote(
                phi.at[:, slab(s)], phi.at[:, slab(s)], 9 + 3 * i + d - 1, 9 + 3 * i + d - 1,
                (b, ((plane + d) % 4) * 2 + ylo),
            )
            cp.start()
            spread.append(cp)

    kernel_keep.wait()
    for cp in kernel_first:
        cp.wait_recv()
    kernel_second = []
    for d in (1, 3, 2):
        cp = remote(kp.at[:, x, kx_half], kp.at[:, x, kx_half], 15 + d, 15 + d, ((b + 4 * d) % 16, q))
        cp.start()
        kernel_second.append(cp)
    for cp in kernel_second:
        cp.wait_recv()
    kernel_third = remote(kp.at[:, :, kx_half], kp.at[:, :, kx_half], 19, 19, sibling)
    kernel_third.start()

    for cp in spread:
        cp.wait_recv()

    owner = core == plane // 2
    held = phi.at[plane % 2]
    target_keep = pltpu.make_async_copy(held, targ.at[0], local.at[2])
    target_give = remote(held, targ.at[0], 20, 20, sibling)

    @pl.when(owner)
    def _():
        target_give.start()
        target_keep.start()
        target_keep.wait()

    @pl.when(jnp.logical_not(owner))
    def _():
        target_give.wait_recv()

    half = pl.ds(pl.multiple_of(core * 2048, 128), 2048)
    halo = []
    for n in (1, 2):
        cp = remote(targ.at[0, :, :, half], targ.at[n, :, :, half], 20 + n, 20 + n, device(chip - n, core, plane))
        cp.start()
        halo.append(cp)

    kernel_third.wait_recv()
    unpack_kernel(kp, kern)

    def transform(n, hook_a, hook_b):
        forward_columns(targ.at[n], phi, fx, z)
        forward_rows(tw, z)
        hook_a()
        middle(kern, fz, iz, z)
        hook_b()
        inverse_rows(tw, z)
        inverse_columns(phi, ix, z, part.at[n])

    swap = []
    for n in (1, 2):
        swap.append(remote(targ.at[n, :, :, half], targ.at[n, :, :, half], 22 + n, 22 + n, sibling))

    def pass_on():
        for n in (1, 2):
            halo[n - 1].wait_recv()
            swap[n - 1].start()

    core_sum = [remote(part.at[n, 1 - core], rcore.at[n], 25 + n, 25 + n, sibling) for n in range(3)]
    halo_sum = [
        remote(part.at[n, core], rhalo.at[n - 1], 27 + n, 27 + n, device(chip + n, core, plane)) for n in (1, 2)
    ]

    def add_core(n):
        core_sum[n].wait_recv()

        @pl.loop(0, 4)
        def _(i):
            part[n, core, i] = part[n, core, i] + rcore[n, i]

    nothing = lambda: None
    transform(0, nothing, pass_on)
    core_sum[0].start()
    swap[0].wait_recv()

    transform(1, functools.partial(add_core, 0), nothing)
    core_sum[1].start()
    swap[1].wait_recv()

    def send_one():
        add_core(1)
        halo_sum[0].start()

    transform(2, send_one, nothing)
    core_sum[2].start()
    add_core(2)
    halo_sum[1].start()

    for n in (1, 2):
        halo_sum[n - 1].wait_recv()

    @pl.loop(0, 4)
    def _(i):
        total[i] = part[0, core, i] + rhalo[0, i] + rhalo[1, i]

    last = []
    for d in range(4):
        zz = (plane + d) % 4
        cp = remote(total.at[zz], out.at[plane], 30 + d, 30 + d, (block * 2 + ylo, zz * 2 + core))
        if d == 0:
            result_keep = pltpu.make_async_copy(total.at[zz], out.at[plane], local.at[3])

            @pl.when(mine)
            def _():
                result_keep.start()
                result_keep.wait()

            @pl.when(jnp.logical_not(mine))
            def _():
                cp.start()
                cp.wait()
        else:
            cp.start()
            last.append(cp)
    for cp in last:
        cp.wait()

    @pl.when(jnp.logical_not(mine))
    def _():
        keep_remote.wait_send()

    @pl.when(owner)
    def _():
        target_give.wait_send()

    for cp in [first_send, kernel_third] + kernel_first + kernel_second + spread + halo + swap + core_sum + halo_sum:
        cp.wait_send()


def local(orbitals, kernel):
    packed = jnp.transpose(kernel, (1, 0, 2))
    packed = jnp.concatenate([packed[:4], packed[4:]], -1)
    vmem = pl.BlockSpec(memory_space=pltpu.VMEM)
    return pl.pallas_call(
        body,
        out_shape=jax.ShapeDtypeStruct(orbitals.shape, F32),
        in_specs=[vmem] * 7,
        out_specs=vmem,
        scratch_shapes=[
            pltpu.VMEM((2, 8, 8, 4096), F32),
            pltpu.VMEM((3, 8, 8, 4096), F32),
            pltpu.VMEM((8, 4, 64, 128), F32),
            pltpu.VMEM((32, 64, 128), F32),
            pltpu.VMEM((32, 128, 128), F32),
            pltpu.VMEM((3, 2, 4, 8, 4096), F32),
            pltpu.VMEM((3, 4, 8, 4096), F32),
            pltpu.VMEM((2, 4, 8, 4096), F32),
            pltpu.VMEM((4, 8, 4096), F32),
            pltpu.SemaphoreType.DMA((34,)),
            pltpu.SemaphoreType.DMA((34,)),
            pltpu.SemaphoreType.DMA((4,)),
        ],
        compiler_params=pltpu.CompilerParams(
            collective_id=0, has_side_effects=True, vmem_limit_bytes=52 * 2**20
        ),
    )(orbitals, packed, *[jnp.asarray(table) for table in tables()])


def solution(mesh):
    return jax.shard_map(
        local,
        mesh=mesh,
        in_specs=(P("band", "grid", None), P(None, "grid", None)),
        out_specs=P("band", "grid", None),
        check_vma=False,
    )
```

```python
import math

import jax
import jax.numpy as jnp
import ml_dtypes
import numpy as np
from jax import lax
from jax.experimental import pallas as pl
from jax.experimental.pallas import tpu as pltpu
from jax.sharding import PartitionSpec as P

G = 64
BF = jnp.bfloat16
F32 = jnp.float32
H = math.sqrt(0.5)
MESH = pl.DeviceIdType.MESH
YA = 16


def split_table(matrix):
    hi = matrix.astype(ml_dtypes.bfloat16)
    return hi, (matrix - hi.astype(np.float64)).astype(ml_dtypes.bfloat16)


def tables():
    k = np.arange(G)
    angle = 2.0 * np.pi * ((k[:, None] * k[None, :]) % G) / G
    c, s = np.cos(angle), np.sin(angle)

    def left(matrix):
        hi, lo = split_table(matrix)
        return np.concatenate([hi, hi, lo], 1)

    def right(matrix):
        hi, lo = split_table(matrix)
        return np.concatenate([hi, hi, lo], 0)

    forward_x = left(np.block([[c, s], [-s, c]]))
    inverse_x = left(np.block([[c, -s], [s, c]]))
    parity = np.array([[1.0, 1.0], [1.0, -1.0]])
    cc, ss = np.kron(parity, c), np.kron(parity, s)
    forward_z = right(np.block([[cc, -ss], [ss, cc]]))
    inverse_z = right(np.block([[cc, ss], [-ss, cc]]) * (-1.0 / G**3))
    twiddle = np.ones((32, 2, 8, 128), np.float64)
    turn = 2.0 * np.pi * np.arange(32) / G
    twiddle[:, 0, :, 64:] = np.cos(turn)[:, None, None]
    twiddle[:, 1, :, :64] = 0.0
    twiddle[:, 1, :, 64:] = np.sin(turn)[:, None, None]
    return forward_x, inverse_x, forward_z, inverse_z, twiddle.astype(np.float32)


def cadd(a, b):
    return a[0] + b[0], a[1] + b[1]


def csub(a, b):
    return a[0] - b[0], a[1] - b[1]


def rot(a, sign):
    return (-a[1], a[0]) if sign > 0 else (a[1], -a[0])


def dft4(v, sign):
    p, q = cadd(v[0], v[2]), csub(v[0], v[2])
    r, t = cadd(v[1], v[3]), csub(v[1], v[3])
    t = rot(t, sign)
    return [cadd(p, r), cadd(q, t), csub(p, r), csub(q, t)]


def dft8(v, sign):
    e = dft4(v[0::2], sign)
    o = dft4(v[1::2], sign)
    a, b = o[1], o[3]
    if sign > 0:
        o[1] = (H * (a[0] - a[1]), H * (a[0] + a[1]))
        o[3] = (-H * (b[0] + b[1]), H * (b[0] - b[1]))
    else:
        o[1] = (H * (a[0] + a[1]), H * (a[1] - a[0]))
        o[3] = (H * (b[1] - b[0]), -H * (b[0] + b[1]))
    o[2] = rot(o[2], sign)
    return [cadd(e[i], o[i]) for i in range(4)] + [csub(e[i], o[i]) for i in range(4)]


def dft32(load, store, sign):
    mid = {}
    for n2 in range(4):
        out = dft8([load(4 * n1 + n2) for n1 in range(8)], sign)
        for k1 in range(8):
            v = out[k1]
            if n2 * k1 == 4:
                v = (H * (v[0] - sign * v[1]), H * (v[1] + sign * v[0]))
            elif n2 * k1:
                turn = sign * 2.0 * math.pi * n2 * k1 / 32
                c, s = math.cos(turn), math.sin(turn)
                v = (v[0] * c - v[1] * s, v[0] * s + v[1] * c)
            mid[n2, k1] = v
    for k1 in range(8):
        out = dft4([mid[n2, k1] for n2 in range(4)], sign)
        for k2 in range(4):
            store(k1 + 8 * k2, out[k2])


def split(x):
    hi = x.astype(BF)
    return hi, (x - hi.astype(F32)).astype(BF)


def dot(a, b):
    return jnp.dot(a, b, preferred_element_type=F32)


def forward_slabs(active, targ, phi, fz, tw, z, s):
    count = len(active)

    def pick(u, values):
        total, chosen, row = values[0], 1, list(values)
        for order in range(1, count):
            row = [after - before for before, after in zip(row, row[1:])]
            chosen = chosen * (u - order + 1)
            total = total + row[0] * (chosen // math.factorial(order))
        return total

    @pl.loop(0, count)
    def _(u):
        n = pick(u, [n for n, _ in active])
        slab = pick(u, [slab for _, slab in active])

        def load(y):
            at = slice(128 * y, 128 * (y + 1))
            t = targ[n, slab, :, at]
            return t * phi[0, slab, :, at], t * phi[1, slab, :, at]

        def store(k, v):
            c, w = tw[k, 0], tw[k, 1]
            s[u, k, :, 0:128] = v[0] * c + v[1] * w
            s[u, k, :, 128:256] = v[1] * c - v[0] * w

        dft32(load, store, -1)

    hi, lo = split(s[0:count].reshape(count * 256, 256))
    res = dot(jnp.concatenate([hi, lo, hi], 1), fz[...])
    for u, (n, slab) in enumerate(active):
        part = res[256 * u : 256 * (u + 1)]
        base = pl.multiple_of(8 * slab, 8)
        z[n, :, pl.ds(base, 8), :] = part[:, :128].reshape(32, 8, 128)
        z[n, :, pl.ds(64 + base, 8), :] = part[:, 128:].reshape(32, 8, 128)


def middle(n, kern, fx, ix, z):
    @pl.loop(0, 32 // YA)
    def _(step):
        ks = [step * YA + i for i in range(YA)]
        hi, lo = split(jnp.concatenate([z[n, k] for k in ks], 1))
        res = dot(fx[...], jnp.concatenate([hi, lo, hi], 0))
        kv = jnp.concatenate([kern[k] for k in ks], 1)
        hi, lo = split(res * jnp.concatenate([kv, kv], 0))
        res = dot(ix[...], jnp.concatenate([hi, lo, hi], 0))
        for i in range(YA):
            z[n, step * YA + i] = res[:, 128 * i : 128 * (i + 1)]


def inverse_slabs(n, parity, phi, iz, tw, z, s, part):
    rows = []
    for zz in range(4):
        base = pl.multiple_of(16 * zz + 8 * parity, 8)
        re = z[n, :, pl.ds(base, 8), :].reshape(256, 128)
        im = z[n, :, pl.ds(64 + base, 8), :].reshape(256, 128)
        rows.append(jnp.concatenate([re, im], 1))
    hi, lo = split(jnp.concatenate(rows, 0))
    s[...] = dot(jnp.concatenate([hi, lo, hi], 1), iz[...]).reshape(4, 32, 8, 256)

    @pl.loop(0, 4)
    def _(zz):
        slab = 2 * zz + parity

        def load(k):
            c, w = tw[k, 0], tw[k, 1]
            r, i = s[zz, k, :, 0:128], s[zz, k, :, 128:256]
            return r * c - i * w, i * c + r * w

        def store(y, v):
            at = slice(128 * y, 128 * (y + 1))
            part[zz, :, at] = v[0] * phi[0, slab, :, at] + v[1] * phi[1, slab, :, at]

        dft32(load, store, 1)


def unpack_kernel(kp, kern):
    low = lax.broadcasted_iota(jnp.int32, (64, 128), 1) < 64

    @pl.loop(0, 4)
    def _(slab):
        @pl.loop(0, 4)
        def _(r):
            a, b = kp[slab, r], kp[slab + 4, r]
            kern[slab * 8 + r] = jnp.where(low, a, pltpu.roll(b, 64, 1))
            kern[slab * 8 + 4 + r] = jnp.where(low, pltpu.roll(a, 64, 1), b)


def body(
    orb, kernel, fx_in, ix_in, fz_in, iz_in, tw_in, out,
    phi, targ, kslab, kpk, kp, kern, z, s, part, rcore, acc, fx, ix, fz, iz, tw, send, recv, local,
):
    b = lax.axis_index("band")
    q = lax.axis_index("grid")
    core, block, x = b % 2, b // 2, b // 4
    plane, ylo = q // 2, q % 2
    odd = (ylo + block) % 2
    home = (core + block) % 2
    chip = block * 2 + odd
    sibling = (block * 2 + 1 - core, q)
    near = (b, plane * 2 + 1 - ylo)
    mine = core == odd
    owner = core == plane // 2

    def device(h, c, zz):
        h = (h + 16) % 16
        return ((h // 2) * 2 + c, zz * 2 + (h + h // 2) % 2)

    def at_plane(d):
        return (b, ((plane + d) % 4) * 2 + ylo)

    def result_device(n, zz):
        return ((chip + n) % 16, zz * 2 + home)

    count = [0]

    def slots(n):
        count[0] += n
        return count[0] - n

    def remote(src, dst, s, where, r=None):
        return pltpu.make_async_remote_copy(
            src_ref=src, dst_ref=dst, send_sem=send.at[s], recv_sem=recv.at[s if r is None else r],
            device_id=where, device_id_type=MESH,
        )

    sent, sent_owner = [], []

    def start(cp):
        cp.start()
        sent.append(cp)

    loads = [
        pltpu.make_async_copy(src, dst, local.at[i])
        for i, (src, dst) in enumerate(
            [(kernel, kslab), (fx_in, fx), (ix_in, ix), (fz_in, fz), (iz_in, iz), (tw_in, tw)]
        )
    ]
    for cp in loads:
        cp.start()

    barrier = pltpu.get_barrier_semaphore()
    greeted = []
    for dc in range(2):
        for dq in range(8):
            if dc or dq:
                greeted.append(((b + dc) % 2 + block * 2, (q + dq) % 8))
    greeted.append(device(chip - 2, core, plane))
    greeted.append(device(chip + 2, core, plane))
    for n in (1, 2):
        for zz in range(4):
            greeted.append(result_device(n, zz))
            behind = (b - n + 16) % 16
            greeted.append(device(behind, (ylo + behind // 2) % 2, zz))
    for dx in (4, 8, 12):
        greeted.append(((b + dx) % 16, q))
    for where in greeted:
        pl.semaphore_signal(barrier, inc=1, device_id=where, device_id_type=MESH)
    pl.semaphore_wait(barrier, len(greeted))

    s_first = slots(4)
    firsts = {}
    for k in range(2):
        for dc in range(2):
            c = (core + dc) % 2
            src, dst = orb.at[2 * c + k], phi.at[k, q]
            firsts[dc, k] = remote(src, dst, s_first + 2 * dc + k, (block * 2 + c, plane * 2 + home), s_first + 2 * ylo + k)
    keeps = [pltpu.make_async_copy(orb.at[2 * core + k], phi.at[k, q], local.at[6 + k]) for k in range(2)]
    for k in range(2):

        @pl.when(mine)
        def _():
            keeps[k].start()

        @pl.when(jnp.logical_not(mine))
        def _():
            firsts[0, k].start()

        start(firsts[1, k])

    def wait_first(i):
        p = (ylo + i) % 2
        for k in range(2):
            piece = phi.at[k, 2 * plane + p]
            cp = remote(piece, piece, s_first, (b, q), s_first + 2 * p + k)
            if i == 0:

                @pl.when(mine)
                def _():
                    keeps[k].wait()

                @pl.when(jnp.logical_not(mine))
                def _():
                    cp.wait_recv()
            else:
                cp.wait_recv()

    s_step = slots(8)
    s_pass = slots(4)

    def slab_at(d, i):
        return ((plane + d) % 4) * 2 + (ylo + i) % 2

    def step_copy(i, side, k):
        d = (1, 3)[side]
        piece = phi.at[k, slab_at(0, i)]
        return remote(piece, piece, s_step + 4 * i + 2 * side + k, at_plane(d))

    def step_wait(i, side, k):
        piece = phi.at[k, slab_at((3, 1)[side], i)]
        remote(piece, piece, s_step, (b, q), s_step + 4 * i + 2 * side + k).wait_recv()

    def pass_copy(i, k):
        piece = phi.at[k, slab_at((3, 1)[i], i)]
        return remote(piece, piece, s_pass + 2 * i + k, at_plane((1, 3)[i]))

    def pass_wait(i, k):
        piece = phi.at[k, slab_at(2, i)]
        remote(piece, piece, s_pass, (b, q), s_pass + 2 * i + k).wait_recv()

    def step_start(i, side):
        d = (1, 3)[side]
        for turn in range(2):
            start(step_copy(i, side, (plane + d + turn) % 2))

    s_t0 = slots(8)
    s_t1 = slots(8)
    s_t2 = slots(8)
    s_t1_give = slots(8)
    s_t2_give = slots(8)
    order = [(0, 0), (3, 0), (1, 0), (0, 1), (2, 0), (1, 1), (3, 1), (2, 1)]
    kt = plane % 2
    far_back = device(chip - 2, core, plane)

    def target_slab(n, j):
        d, i = order[j]
        flip = (0, 1 - odd, 1)[n]
        return ((plane + d) % 4) * 2 + (ylo + flip + i) % 2

    def own_target(j):
        s = target_slab(0, j)
        src = phi.at[kt, s]
        keep = pltpu.make_async_copy(src, targ.at[0, s], local.at[8 + j])
        give = remote(src, targ.at[0, s], s_t0 + j, sibling)
        back = remote(src, targ.at[2, s], s_t2 + j, far_back)
        beside = remote(src, targ.at[1, s], s_t1 + j, near)
        return keep, give, back, beside

    def target_ready(j):
        @pl.when(owner)
        def _():
            keep, give, back, beside = own_target(j)
            back.start()

            @pl.when(odd == 1)
            def _():
                beside.start()

            give.start()
            keep.start()

    def far_target(j):
        s = target_slab(2, j)
        piece = targ.at[2, s]
        arrive = remote(piece, piece, s_t2, (b, q), s_t2 + j)
        beside = remote(piece, targ.at[1, s], s_t1 + j, near)
        give = remote(piece, piece, s_t2_give + j, sibling)
        return arrive, beside, give

    def far_ready(j):
        @pl.when(owner)
        def _():
            arrive, beside, give = far_target(j)
            arrive.wait_recv()

            @pl.when(odd == 0)
            def _():
                beside.start()

            give.start()

    def near_target(j):
        piece = targ.at[1, target_slab(1, j)]
        return remote(piece, piece, s_t1, (b, q), s_t1 + j), remote(piece, piece, s_t1_give + j, sibling)

    def near_ready(j):
        @pl.when(owner)
        def _():
            arrive, give = near_target(j)
            arrive.wait_recv()
            give.start()

    def wait_target(n, j):
        base = (s_t0, s_t1_give, s_t2_give)[n]

        @pl.when(jnp.logical_not(owner))
        def _():
            piece = targ.at[n, target_slab(n, j)]
            remote(piece, piece, base, (b, q), base + j).wait_recv()

        if n == 0:

            @pl.when(owner)
            def _():
                own_target(j)[0].wait()

    s_kernel = slots(11)
    kx_half = pl.ds(pl.multiple_of(32 * core, 32), 32)
    kernel_first = [
        remote(kpk.at[x, kx_half], kp.at[q, x, kx_half], s_kernel + d - 1, (b, (q + d) % 8)) for d in range(1, 8)
    ]
    kernel_second = [
        remote(kp.at[:, x, kx_half], kp.at[:, x, kx_half], s_kernel + 6 + d, ((b + 4 * d) % 16, q)) for d in (1, 3, 2)
    ]
    kernel_third = remote(kp.at[:, :, kx_half], kp.at[:, :, kx_half], s_kernel + 10, sibling)

    def pack_kernel():
        loads[0].wait()
        for r in range(4):
            kpk[r] = jnp.concatenate([kslab[:, r, :], kslab[:, r + 4, :]], 1)
        for cp in kernel_first:
            start(cp)
        kp[q, x, kx_half] = kpk[x, kx_half]

    far_steps = {3: (0,), 5: (2, 3), 6: (1,), 7: (4, 5), 8: (6,), 9: (7,)}
    near_steps = {3: (0,), 5: (2,), 6: (1, 3), 7: (4,), 8: (5,), 9: (6,), 10: (7,)}

    def forward(j):
        if 2 <= j < 10:
            far_ready(j - 2)
        if 3 <= j < 11:
            near_ready(j - 3)
        active = [(0, j)] if j < 8 else []
        active += [(2, i) for i in far_steps.get(j, ())] + [(1, i) for i in near_steps.get(j, ())]
        for n, i in active:
            wait_target(n, i)
        active = [(n, target_slab(n, i)) for n, i in active]
        forward_slabs(active, targ, phi, fz, tw, z, s)

    wait_first(0)
    step_start(0, 0)
    step_start(0, 1)
    target_ready(0)
    pack_kernel()
    for cp in loads[1:]:
        cp.wait()
    forward(0)
    step_wait(0, 0, kt)
    start(pass_copy(0, kt))
    target_ready(1)
    step_wait(0, 0, 1 - kt)
    start(pass_copy(0, 1 - kt))
    forward(1)
    step_wait(0, 1, kt)
    target_ready(2)
    step_wait(0, 1, 1 - kt)
    wait_first(1)
    step_start(1, 1)
    step_start(1, 0)
    target_ready(3)
    for cp in kernel_first:
        cp.wait_recv()
    for cp in kernel_second:
        start(cp)
    forward(2)
    forward(3)
    pass_wait(0, kt)
    target_ready(4)
    pass_wait(0, 1 - kt)
    step_wait(1, 1, kt)
    start(pass_copy(1, kt))
    target_ready(5)
    step_wait(1, 1, 1 - kt)
    start(pass_copy(1, 1 - kt))
    forward(4)
    for cp in kernel_second:
        cp.wait_recv()
    start(kernel_third)
    forward(5)
    step_wait(1, 0, kt)
    target_ready(6)
    step_wait(1, 0, 1 - kt)
    forward(6)
    kernel_third.wait_recv()
    unpack_kernel(kp, kern)
    pass_wait(1, kt)
    target_ready(7)
    pass_wait(1, 1 - kt)
    forward(7)
    middle(0, kern, fx, ix, z)
    forward(8)
    forward(9)
    forward(10)

    s_core = slots(3)
    s_result = slots(12)

    def core_sum(n):
        return remote(part.at[n, 0], rcore.at[n], s_core + n, sibling)

    def result(n, d):
        zz = (plane + d) % 4
        return remote(part.at[n, 1, zz], acc.at[n, plane], s_result + 4 * n + d, result_device(n, zz))

    result_keep = pltpu.make_async_copy(part.at[0, 1, plane], acc.at[0, plane], local.at[16])

    @pl.loop(0, 3)
    def _(u):
        n = 2 - u

        @pl.when(n > 0)
        def _():
            middle(n, kern, fx, ix, z)

        @pl.loop(0, 2)
        def _(g):
            inverse_slabs(n, (home + 1 + g) % 2, phi, iz, tw, z, s, part.at[n, g])

            @pl.when(g == 0)
            def _():
                core_sum(n).start()

        core_sum(n).wait_recv()

        @pl.loop(0, 4)
        def _(i):
            part[n, 1, i] = part[n, 1, i] + rcore[n, i]

        for d in (2, 1, 3):
            result(n, d).start()

        @pl.when(jnp.logical_or(n > 0, jnp.logical_not(mine)))
        def _():
            result(n, 0).start()

    @pl.when(mine)
    def _():
        result_keep.start()
        result_keep.wait()

    for n in (2, 1, 0):
        for d in range(4):
            if n == 0 and d == 0:

                @pl.when(jnp.logical_not(mine))
                def _():
                    result(0, 0).wait()
            else:
                result(n, d).wait()
        core_sum(n).wait_send()

    @pl.loop(0, 4)
    def _(i):
        out[i] = acc[0, i] + acc[1, i] + acc[2, i]

    for cp in sent:
        cp.wait_send()

    @pl.when(jnp.logical_not(mine))
    def _():
        for k in range(2):
            firsts[0, k].wait_send()

    @pl.when(owner)
    def _():
        for j in range(8):
            keep, give, back, beside = own_target(j)
            give.wait_send()
            back.wait_send()
            arrive, relay, give = far_target(j)
            give.wait_send()
            near_target(j)[1].wait_send()

            @pl.when(odd == 1)
            def _():
                beside.wait_send()

            @pl.when(odd == 0)
            def _():
                relay.wait_send()


def local(orbitals, kernel):
    vmem = pl.BlockSpec(memory_space=pltpu.VMEM)
    anywhere = pl.BlockSpec(memory_space=pl.ANY)
    constants = [jnp.asarray(table) for table in tables()]
    return pl.pallas_call(
        body,
        out_shape=jax.ShapeDtypeStruct(orbitals.shape, F32),
        in_specs=[anywhere] * 7,
        out_specs=vmem,
        scratch_shapes=[
            pltpu.VMEM((2, 8, 8, 4096), F32),
            pltpu.VMEM((3, 8, 8, 4096), F32),
            pltpu.VMEM((64, 8, 64), F32),
            pltpu.VMEM((4, 64, 128), F32),
            pltpu.VMEM((8, 4, 64, 128), F32),
            pltpu.VMEM((32, 64, 128), F32),
            pltpu.VMEM((3, 32, 128, 128), F32),
            pltpu.VMEM((4, 32, 8, 256), F32),
            pltpu.VMEM((3, 2, 4, 8, 4096), F32),
            pltpu.VMEM((3, 4, 8, 4096), F32),
            pltpu.VMEM((3, 4, 8, 4096), F32),
        ]
        + [pltpu.VMEM(table.shape, table.dtype) for table in constants]
        + [
            pltpu.SemaphoreType.DMA((84,)),
            pltpu.SemaphoreType.DMA((84,)),
            pltpu.SemaphoreType.DMA((17,)),
        ],
        compiler_params=pltpu.CompilerParams(
            collective_id=0, has_side_effects=True, vmem_limit_bytes=56 * 2**20
        ),
    )(orbitals, kernel, *constants)


def solution(mesh):
    return jax.shard_map(
        local,
        mesh=mesh,
        in_specs=(P("band", "grid", None), P(None, "grid", None)),
        out_specs=P("band", "grid", None),
        check_vma=False,
    )
```

```python
import math

import jax
import jax.numpy as jnp
import ml_dtypes
import numpy as np
from jax import lax
from jax.experimental import pallas as pl
from jax.experimental.pallas import tpu as pltpu
from jax.sharding import PartitionSpec as P

G = 64
BF = jnp.bfloat16
F32 = jnp.float32
H = math.sqrt(0.5)
MESH = pl.DeviceIdType.MESH
YA = 16
RELAYED = (0, 1, 2, 3, 4, 5, 6, 7)


def split_table(matrix):
    hi = matrix.astype(ml_dtypes.bfloat16)
    return hi, (matrix - hi.astype(np.float64)).astype(ml_dtypes.bfloat16)


def tables():
    k = np.arange(G)
    angle = 2.0 * np.pi * ((k[:, None] * k[None, :]) % G) / G
    c, s = np.cos(angle), np.sin(angle)

    def left(matrix):
        hi, lo = split_table(matrix)
        return np.concatenate([hi, hi, lo], 1)

    def right(matrix):
        hi, lo = split_table(matrix)
        return np.concatenate([hi, hi, lo], 0)

    forward_x = left(np.block([[c, s], [-s, c]]))
    inverse_x = left(np.block([[c, -s], [s, c]]))
    parity = np.array([[1.0, 1.0], [1.0, -1.0]])
    cc, ss = np.kron(parity, c), np.kron(parity, s)
    forward_z = right(np.block([[cc, -ss], [ss, cc]]))
    inverse_z = right(np.block([[cc, ss], [-ss, cc]]) * (-1.0 / G**3))
    twiddle = np.ones((32, 2, 8, 128), np.float64)
    turn = 2.0 * np.pi * np.arange(32) / G
    twiddle[:, 0, :, 64:] = np.cos(turn)[:, None, None]
    twiddle[:, 1, :, :64] = 0.0
    twiddle[:, 1, :, 64:] = np.sin(turn)[:, None, None]
    return forward_x, inverse_x, forward_z, inverse_z, twiddle.astype(np.float32)


def cadd(a, b):
    return a[0] + b[0], a[1] + b[1]


def csub(a, b):
    return a[0] - b[0], a[1] - b[1]


def rot(a, sign):
    return (-a[1], a[0]) if sign > 0 else (a[1], -a[0])


def dft4(v, sign):
    p, q = cadd(v[0], v[2]), csub(v[0], v[2])
    r, t = cadd(v[1], v[3]), csub(v[1], v[3])
    t = rot(t, sign)
    return [cadd(p, r), cadd(q, t), csub(p, r), csub(q, t)]


def dft8(v, sign):
    e = dft4(v[0::2], sign)
    o = dft4(v[1::2], sign)
    a, b = o[1], o[3]
    if sign > 0:
        o[1] = (H * (a[0] - a[1]), H * (a[0] + a[1]))
        o[3] = (-H * (b[0] + b[1]), H * (b[0] - b[1]))
    else:
        o[1] = (H * (a[0] + a[1]), H * (a[1] - a[0]))
        o[3] = (H * (b[1] - b[0]), -H * (b[0] + b[1]))
    o[2] = rot(o[2], sign)
    return [cadd(e[i], o[i]) for i in range(4)] + [csub(e[i], o[i]) for i in range(4)]


def dft32(load, store, sign):
    mid = {}
    for n2 in range(4):
        out = dft8([load(4 * n1 + n2) for n1 in range(8)], sign)
        for k1 in range(8):
            v = out[k1]
            if n2 * k1 == 4:
                v = (H * (v[0] - sign * v[1]), H * (v[1] + sign * v[0]))
            elif n2 * k1:
                turn = sign * 2.0 * math.pi * n2 * k1 / 32
                c, s = math.cos(turn), math.sin(turn)
                v = (v[0] * c - v[1] * s, v[0] * s + v[1] * c)
            mid[n2, k1] = v
    for k1 in range(8):
        out = dft4([mid[n2, k1] for n2 in range(4)], sign)
        for k2 in range(4):
            store(k1 + 8 * k2, out[k2])


def split(x):
    hi = x.astype(BF)
    return hi, (x - hi.astype(F32)).astype(BF)


def dot(a, b):
    return jnp.dot(a, b, preferred_element_type=F32)


def forward_slabs(active, targ, phi, fz, tw, z, s):
    count = len(active)

    def pick(u, values):
        total, chosen, row = values[0], 1, list(values)
        for order in range(1, count):
            row = [after - before for before, after in zip(row, row[1:])]
            chosen = chosen * (u - order + 1)
            total = total + row[0] * (chosen // math.factorial(order))
        return total

    @pl.loop(0, count)
    def _(u):
        n = pick(u, [n for n, _ in active])
        slab = pick(u, [slab for _, slab in active])

        def load(y):
            at = slice(128 * y, 128 * (y + 1))
            t = targ[n, slab, :, at]
            return t * phi[0, slab, :, at], t * phi[1, slab, :, at]

        def store(k, v):
            c, w = tw[k, 0], tw[k, 1]
            s[u, k, :, 0:128] = v[0] * c + v[1] * w
            s[u, k, :, 128:256] = v[1] * c - v[0] * w

        dft32(load, store, -1)

    hi, lo = split(s[0:count].reshape(count * 256, 256))
    res = dot(jnp.concatenate([hi, lo, hi], 1), fz[...])
    for u, (n, slab) in enumerate(active):
        part = res[256 * u : 256 * (u + 1)]
        base = pl.multiple_of(8 * slab, 8)
        z[n, :, pl.ds(base, 8), :] = part[:, :128].reshape(32, 8, 128)
        z[n, :, pl.ds(64 + base, 8), :] = part[:, 128:].reshape(32, 8, 128)


def middle(n, kern, fx, ix, z):
    @pl.loop(0, 32 // YA)
    def _(step):
        ks = [step * YA + i for i in range(YA)]
        hi, lo = split(jnp.concatenate([z[n, k] for k in ks], 1))
        res = dot(fx[...], jnp.concatenate([hi, lo, hi], 0))
        kv = jnp.concatenate([kern[k] for k in ks], 1)
        hi, lo = split(res * jnp.concatenate([kv, kv], 0))
        res = dot(ix[...], jnp.concatenate([hi, lo, hi], 0))
        for i in range(YA):
            z[n, step * YA + i] = res[:, 128 * i : 128 * (i + 1)]


def inverse_slabs(n, parity, phi, iz, tw, z, s, part):
    rows = []
    for zz in range(4):
        base = pl.multiple_of(16 * zz + 8 * parity, 8)
        re = z[n, :, pl.ds(base, 8), :].reshape(256, 128)
        im = z[n, :, pl.ds(64 + base, 8), :].reshape(256, 128)
        rows.append(jnp.concatenate([re, im], 1))
    hi, lo = split(jnp.concatenate(rows, 0))
    s[0:4] = dot(jnp.concatenate([hi, lo, hi], 1), iz[...]).reshape(4, 32, 8, 256)

    @pl.loop(0, 4)
    def _(zz):
        slab = 2 * zz + parity

        def load(k):
            c, w = tw[k, 0], tw[k, 1]
            r, i = s[zz, k, :, 0:128], s[zz, k, :, 128:256]
            return r * c - i * w, i * c + r * w

        def store(y, v):
            at = slice(128 * y, 128 * (y + 1))
            part[zz, :, at] = v[0] * phi[0, slab, :, at] + v[1] * phi[1, slab, :, at]

        dft32(load, store, 1)


def unpack_kernel(kp, kern):
    low = lax.broadcasted_iota(jnp.int32, (64, 128), 1) < 64

    @pl.loop(0, 4)
    def _(slab):
        @pl.loop(0, 4)
        def _(r):
            a, b = kp[slab, r], kp[slab + 4, r]
            kern[slab * 8 + r] = jnp.where(low, a, pltpu.roll(b, 64, 1))
            kern[slab * 8 + 4 + r] = jnp.where(low, pltpu.roll(a, 64, 1), b)


def body(
    orb, kernel, fx_in, ix_in, fz_in, iz_in, tw_in, out,
    phi, targ, kslab, kpk, kp, kern, z, s, part, rcore, acc, extra, fx, ix, fz, iz, tw, send, recv, local,
):
    b = lax.axis_index("band")
    q = lax.axis_index("grid")

    def mod(value, n):
        return lax.rem(value, jnp.int32(n))

    def div(value, n):
        return lax.div(value, jnp.int32(n))

    core, block, x = mod(b, 2), div(b, 2), div(b, 4)
    plane, ylo = div(q, 2), mod(q, 2)
    odd = mod(ylo + block, 2)
    home = mod(core + block, 2)
    chip = block * 2 + odd
    sibling = (block * 2 + 1 - core, q)
    near = (b, plane * 2 + 1 - ylo)
    mine = core == odd
    owner = core == div(plane, 2)
    planes = [plane] + [mod(plane + d, 4) for d in (1, 2, 3)]
    parities = [ylo, 1 - ylo]
    slabs = [[2 * zz + p for p in parities] for zz in planes]
    targets_here = [div(zz, 2) == core for zz in planes]
    kt = mod(plane, 2)
    other = 1 - kt
    band_of = [kt, other, kt, other]
    across = [(b, 2 * zz + ylo) for zz in planes]
    near_slabs = [[2 * zz + mod(ylo + 1 - odd + i, 2) for i in range(2)] for zz in planes]

    def device(h, c, zz):
        h = mod(h + 16, 16)
        half = div(h, 2)
        return (half * 2 + c, zz * 2 + mod(h + half, 2))

    def at_plane(d):
        return across[d]

    def result_device(n, zz):
        return (mod(chip + n, 16), zz * 2 + home)

    count = [0]

    def slots(n):
        count[0] += n
        return count[0] - n

    def remote(src, dst, s, where, r=None):
        return pltpu.make_async_remote_copy(
            src_ref=src, dst_ref=dst, send_sem=send.at[s], recv_sem=recv.at[s if r is None else r],
            device_id=where, device_id_type=MESH,
        )

    sent, sent_owner = [], []

    def start(cp):
        cp.start()
        sent.append(cp)

    loads = [
        pltpu.make_async_copy(src, dst, local.at[i])
        for i, (src, dst) in enumerate(
            [(kernel, kslab), (fx_in, fx), (ix_in, ix), (fz_in, fz), (iz_in, iz), (tw_in, tw)]
        )
    ]
    for cp in loads:
        cp.start()

    barrier = pltpu.get_barrier_semaphore()
    greeted = []
    for dc in range(2):
        for dq in range(8):
            if dc or dq:
                greeted.append((mod(b + dc, 2) + block * 2, mod(q + dq, 8)))
    for dh in (-2, -1, 1, 2):
        greeted.append(device(chip + dh, core, plane))
    for n in (1, 2):
        behind = mod(b - n + 16, 16)
        behind_core = mod(ylo + div(behind, 2), 2)
        for zz in range(4):
            greeted.append(result_device(n, zz))
            greeted.append(device(behind, behind_core, zz))
    for dx in (4, 8, 12):
        greeted.append((mod(b + dx, 16), q))
    for where in greeted:
        pl.semaphore_signal(barrier, inc=1, device_id=where, device_id_type=MESH)
    pl.semaphore_wait(barrier, len(greeted))

    s_first = slots(4)
    firsts = {}
    for k in range(2):
        for dc in range(2):
            c = (core, 1 - core)[dc]
            src, dst = orb.at[2 * c + k], phi.at[k, q]
            firsts[dc, k] = remote(src, dst, s_first + 2 * dc + k, (block * 2 + c, plane * 2 + home), s_first + 2 * ylo + k)
    s_direct = slots(6)

    def direct(d):
        k = planes[d]
        slot = s_direct + 2 * d - 2
        return remote(orb.at[k], phi.at[band_of[d], q], slot, (block * 2 + div(k, 2), k * 2 + home), slot + ylo)

    def direct_wait(d, i):
        piece = phi.at[kt, slabs[d][i]]
        remote(piece, piece, s_direct, (b, q), s_direct + 2 * (4 - d) - 2 + parities[i]).wait_recv()

    for d in (1, 3, 2):
        start(direct(d))
    keeps = [pltpu.make_async_copy(orb.at[2 * core + k], phi.at[k, q], local.at[6 + k]) for k in range(2)]
    for k in range(2):

        @pl.when(mine)
        def _():
            keeps[k].start()

        @pl.when(jnp.logical_not(mine))
        def _():
            firsts[0, k].start()

        start(firsts[1, k])

    def wait_first(i):
        p = parities[i]
        for k in range(2):
            piece = phi.at[k, slabs[0][i]]
            cp = remote(piece, piece, s_first, (b, q), s_first + 2 * p + k)
            if i == 0:

                @pl.when(mine)
                def _():
                    keeps[k].wait()

                @pl.when(jnp.logical_not(mine))
                def _():
                    cp.wait_recv()
            else:
                cp.wait_recv()

    s_step = slots(8)
    s_pass = slots(4)

    def slab_at(d, i):
        return slabs[d][i]

    def step_copy(i, side, k):
        d = (1, 3)[side]
        piece = phi.at[k, slab_at(0, i)]
        return remote(piece, piece, s_step + 4 * i + 2 * side + k, at_plane(d))

    def start_it(cp):
        cp.start()

    def wait_sent(cp):
        cp.wait_send()

    def step_wait(i, side, k):
        piece = phi.at[k, slab_at((3, 1)[side], i)]
        remote(piece, piece, s_step, (b, q), s_step + 4 * i + 2 * side + k).wait_recv()

    def pass_copy(i, which):
        side = (i + which) % 2
        piece = phi.at[band_of[which], slab_at((3, 1)[side], i)]
        return remote(piece, piece, s_pass + 2 * i + which, at_plane((1, 3)[side]), s_pass + 2 * i + band_of[which])

    def pass_wait(i, k):
        piece = phi.at[k, slab_at(2, i)]
        remote(piece, piece, s_pass, (b, q), s_pass + 2 * i + k).wait_recv()

    def unless(condition):
        return pl.when(jnp.logical_not(condition))

    def each_other(i, act):
        for side, d in enumerate((1, 3)):
            act(step_copy(i, side, kt))

            @unless(targets_here[d])
            def _():
                act(step_copy(i, side, other))

    def each_pass(i, act):
        act(pass_copy(i, 0))

        @unless(targets_here[(3, 1)[i]])
        def _():
            act(pass_copy(i, 1))

    s_t0 = slots(8)
    s_t1 = slots(8)
    s_t2 = slots(8)
    s_t1_give = slots(8)
    s_t2_give = slots(8)
    order = [(0, 0), (3, 0), (1, 0), (0, 1), (2, 0), (1, 1), (3, 1), (2, 1)]
    far_back = device(chip - 2, core, plane)
    near_back = device(chip - 1, core, plane)

    def target_slab(n, j):
        d, i = order[j]
        return (slabs[d][i], near_slabs[d][i], slabs[d][1 - i])[n]

    def own_target(j):
        s = target_slab(0, j)
        src = phi.at[kt, s]
        keep = pltpu.make_async_copy(src, targ.at[0, s], local.at[8 + j])
        give = remote(src, targ.at[0, s], s_t0 + j, sibling)
        back = remote(src, targ.at[2, s], s_t2 + j, far_back)
        beside = remote(src, targ.at[1, s], s_t1 + j, near_back)
        return keep, give, back, beside

    def target_ready(j):
        @pl.when(owner)
        def _():
            keep, give, back, beside = own_target(j)
            back.start()
            if j in RELAYED:

                @pl.when(odd == 1)
                def _():
                    beside.start()
            else:
                beside.start()
            give.start()
            keep.start()

    def far_target(j):
        s = target_slab(2, j)
        piece = targ.at[2, s]
        arrive = remote(piece, piece, s_t2, (b, q), s_t2 + j)
        relay = remote(piece, targ.at[1, s], s_t1 + j, near)
        give = remote(piece, piece, s_t2_give + j, sibling)
        return arrive, relay, give

    def far_ready(j):
        @pl.when(owner)
        def _():
            arrive, relay, give = far_target(j)
            arrive.wait_recv()
            if j in RELAYED:

                @pl.when(odd == 0)
                def _():
                    relay.start()

            give.start()

    def near_target(j):
        piece = targ.at[1, target_slab(1, j)]
        return remote(piece, piece, s_t1, (b, q), s_t1 + j), remote(piece, piece, s_t1_give + j, sibling)

    def near_ready(j):
        @pl.when(owner)
        def _():
            arrive, give = near_target(j)
            arrive.wait_recv()
            give.start()

    def wait_target(n, j):
        base = (s_t0, s_t1_give, s_t2_give)[n]

        @pl.when(jnp.logical_not(owner))
        def _():
            piece = targ.at[n, target_slab(n, j)]
            remote(piece, piece, base, (b, q), base + j).wait_recv()

        if n == 0:

            @pl.when(owner)
            def _():
                own_target(j)[0].wait()

    s_kernel = slots(11)
    kx_half = pl.ds(pl.multiple_of(32 * core, 32), 32)
    kernel_first = [
        remote(kpk.at[x, kx_half], kp.at[q, x, kx_half], s_kernel + d - 1, (b, mod(q + d, 8))) for d in range(1, 8)
    ]
    kernel_second = [
        remote(kp.at[:, x, kx_half], kp.at[:, x, kx_half], s_kernel + 6 + d, (mod(b + 4 * d, 16), q)) for d in (1, 3, 2)
    ]
    kernel_third = remote(kp.at[:, :, kx_half], kp.at[:, :, kx_half], s_kernel + 10, sibling)

    def pack_kernel():
        for r in range(4):
            kpk[r] = jnp.concatenate([kslab[:, r, :], kslab[:, r + 4, :]], 1)
        for cp in kernel_first:
            start(cp)
        kp[q, x, kx_half] = kpk[x, kx_half]

    def forward(*active):
        for n, j in active:
            wait_target(n, j)
        forward_slabs([(n, target_slab(n, j)) for n, j in active], targ, phi, fz, tw, z, s)

    def near_others(i, side):
        step_wait(i, side, other)

        @unless(owner)
        def _():
            step_wait(i, side, kt)

    def far_others(i):
        pass_wait(i, other)

        @unless(owner)
        def _():
            pass_wait(i, kt)

    def target_here(j):
        @pl.when(owner)
        def _():
            direct_wait(*order[j])

        target_ready(j)

    wait_first(0)
    each_other(0, start_it)
    target_ready(0)
    target_here(1)
    target_here(2)
    loads[0].wait()
    pack_kernel()
    target_here(4)
    target_here(5)
    target_here(6)
    for cp in loads[1:]:
        cp.wait()
    forward((0, 0))
    near_others(0, 0)
    near_others(0, 1)
    each_pass(0, start_it)
    target_here(7)
    wait_first(1)
    each_other(1, start_it)
    target_ready(3)
    far_ready(0)
    forward((0, 1), (0, 2))
    for j in (1, 2, 5, 6, 4):
        far_ready(j)
    forward((0, 3))
    for cp in kernel_first:
        cp.wait_recv()
    for cp in kernel_second:
        start(cp)
    far_ready(7)
    near_others(1, 1)
    near_others(1, 0)
    each_pass(1, start_it)
    far_ready(3)
    far_others(0)
    forward((0, 4), (2, 5), (2, 6), (2, 3))
    for cp in kernel_second:
        cp.wait_recv()
    start(kernel_third)
    forward((0, 5), (0, 6), (2, 7))
    kernel_third.wait_recv()
    unpack_kernel(kp, kern)
    far_others(1)
    forward((0, 7))

    s_core = slots(3)
    s_result = slots(12)

    def core_sum(n):
        return remote(part.at[n, 0], rcore.at[n], s_core + n, sibling)

    def result(n, d):
        zz = planes[d]
        return remote(part.at[n, 1, zz], acc.at[n, plane], s_result + 4 * n + d, result_device(n, zz))

    s_extra = slots(4)
    adds = jnp.logical_and(odd == 0, core == 1)
    gives = jnp.logical_and(odd == 1, core == 1)
    has_near = jnp.logical_or(odd == 1, core == 1)

    def exchange(d):
        return remote(part.at[1, 1, planes[d]], extra.at[planes[d]], s_extra + d, near)

    result_keep = pltpu.make_async_copy(part.at[0, 1, plane], acc.at[0, plane], local.at[16])

    @pl.loop(0, 3)
    def _(u):
        n = mod(2 * u, 3)

        @pl.when(u == 1)
        def _():
            for j in range(8):
                near_ready(j)
            forward((2, 0), (2, 1), (2, 2), (2, 4))

        @pl.when(u == 2)
        def _():
            for j in (0, 4):
                forward((1, j), (1, j + 1), (1, j + 2), (1, j + 3))

        middle(n, kern, fx, ix, z)

        @pl.loop(0, 2)
        def _(g):
            inverse_slabs(n, mod(home + 1 + g, 2), phi, iz, tw, z, s, part.at[n, g])

            @pl.when(g == 0)
            def _():
                core_sum(n).start()

        core_sum(n).wait_recv()

        @pl.loop(0, 4)
        def _(i):
            part[n, 1, i] = part[n, 1, i] + rcore[n, i]

        held = jnp.logical_or(jnp.logical_and(adds, n == 2), jnp.logical_and(gives, n == 1))

        @unless(held)
        def _():
            for d in (2, 1, 3):
                result(n, d).start()

        @unless(jnp.logical_or(held, jnp.logical_and(n == 0, mine)))
        def _():
            result(n, 0).start()

        @pl.when(jnp.logical_and(gives, n == 1))
        def _():
            for d in (2, 1, 3, 0):
                exchange(d).start()

    @pl.when(adds)
    def _():
        for d in (2, 1, 3, 0):
            exchange(d).wait_recv()
            part[2, 1, planes[d]] = part[2, 1, planes[d]] + extra[planes[d]]
            result(2, d).start()

    @pl.when(mine)
    def _():
        result_keep.start()
        result_keep.wait()

    for n in range(3):
        core_sum(n).wait_send()
    for d in range(4):
        result(2, d).wait()
        if d:
            result(0, d).wait()

    @unless(mine)
    def _():
        result(0, 0).wait()

    @pl.when(gives)
    def _():
        for d in range(4):
            exchange(d).wait_send()

    @unless(gives)
    def _():
        for d in range(4):
            result(1, d).wait_send()

    @pl.when(has_near)
    def _():
        for d in range(4):
            result(1, d).wait_recv()

        @pl.loop(0, 4)
        def _(i):
            out[i] = acc[0, i] + acc[1, i] + acc[2, i]

    @unless(has_near)
    def _():
        @pl.loop(0, 4)
        def _(i):
            out[i] = acc[0, i] + acc[2, i]

    for cp in sent:
        cp.wait_send()
    for i in range(2):
        each_other(i, wait_sent)
        each_pass(i, wait_sent)

    @pl.when(jnp.logical_not(mine))
    def _():
        for k in range(2):
            firsts[0, k].wait_send()

    @pl.when(owner)
    def _():
        for j in range(8):
            keep, give, back, beside = own_target(j)
            give.wait_send()
            back.wait_send()
            arrive, relay, pass_on = far_target(j)
            pass_on.wait_send()
            if j in RELAYED:

                @pl.when(odd == 1)
                def _():
                    beside.wait_send()

                @pl.when(odd == 0)
                def _():
                    relay.wait_send()
            else:
                beside.wait_send()
            near_target(j)[1].wait_send()


def local(orbitals, kernel):
    vmem = pl.BlockSpec(memory_space=pltpu.VMEM)
    anywhere = pl.BlockSpec(memory_space=pl.ANY)
    constants = [jnp.asarray(table) for table in tables()]
    return pl.pallas_call(
        body,
        out_shape=jax.ShapeDtypeStruct(orbitals.shape, F32),
        in_specs=[anywhere] * 7,
        out_specs=vmem,
        scratch_shapes=[
            pltpu.VMEM((2, 8, 8, 4096), F32),
            pltpu.VMEM((3, 8, 8, 4096), F32),
            pltpu.VMEM((64, 8, 64), F32),
            pltpu.VMEM((4, 64, 128), F32),
            pltpu.VMEM((8, 4, 64, 128), F32),
            pltpu.VMEM((32, 64, 128), F32),
            pltpu.VMEM((3, 32, 128, 128), F32),
            pltpu.VMEM((5, 32, 8, 256), F32),
            pltpu.VMEM((3, 2, 4, 8, 4096), F32),
            pltpu.VMEM((3, 4, 8, 4096), F32),
            pltpu.VMEM((3, 4, 8, 4096), F32),
            pltpu.VMEM((4, 8, 4096), F32),
        ]
        + [pltpu.VMEM(table.shape, table.dtype) for table in constants]
        + [
            pltpu.SemaphoreType.DMA((92,)),
            pltpu.SemaphoreType.DMA((92,)),
            pltpu.SemaphoreType.DMA((17,)),
        ],
        compiler_params=pltpu.CompilerParams(
            collective_id=0, has_side_effects=True, vmem_limit_bytes=56 * 2**20
        ),
    )(orbitals, kernel, *constants)


def solution(mesh):
    return jax.shard_map(
        local,
        mesh=mesh,
        in_specs=(P("band", "grid", None), P(None, "grid", None)),
        out_specs=P("band", "grid", None),
        check_vma=False,
    )
```

```python
import math

import jax
import jax.numpy as jnp
import ml_dtypes
import numpy as np
from jax import lax
from jax.experimental import pallas as pl
from jax.experimental.pallas import tpu as pltpu
from jax.sharding import PartitionSpec as P

G = 64
BF = jnp.bfloat16
F32 = jnp.float32
H = math.sqrt(0.5)
MESH = pl.DeviceIdType.MESH
YA = 32
RELAYED = (0, 1, 2, 3, 4, 5, 6, 7)


def split_table(matrix):
    hi = matrix.astype(ml_dtypes.bfloat16)
    return hi, (matrix - hi.astype(np.float64)).astype(ml_dtypes.bfloat16)


def tables():
    k = np.arange(G)
    angle = 2.0 * np.pi * ((k[:, None] * k[None, :]) % G) / G
    c, s = np.cos(angle), np.sin(angle)

    def left(matrix):
        hi, lo = split_table(matrix)
        return np.concatenate([hi, hi, lo], 1)

    def right(matrix):
        hi, lo = split_table(matrix)
        return np.concatenate([hi, hi, lo], 0)

    forward_x = left(np.block([[c, s], [-s, c]]))
    inverse_x = left(np.block([[c, -s], [s, c]]))
    parity = np.array([[1.0, 1.0], [1.0, -1.0]])
    cc, ss = np.kron(parity, c), np.kron(parity, s)
    forward_z = right(np.block([[cc, -ss], [ss, cc]]))
    inverse_z = right(np.block([[cc, ss], [-ss, cc]]) * (-1.0 / G**3))
    twiddle = np.ones((32, 2, 8, 128), np.float64)
    turn = 2.0 * np.pi * np.arange(32) / G
    twiddle[:, 0, :, 64:] = np.cos(turn)[:, None, None]
    twiddle[:, 1, :, :64] = 0.0
    twiddle[:, 1, :, 64:] = np.sin(turn)[:, None, None]
    return forward_x, inverse_x, forward_z, inverse_z, twiddle.astype(np.float32)


def cadd(a, b):
    return a[0] + b[0], a[1] + b[1]


def csub(a, b):
    return a[0] - b[0], a[1] - b[1]


def rot(a, sign):
    return (-a[1], a[0]) if sign > 0 else (a[1], -a[0])


def dft4(v, sign):
    p, q = cadd(v[0], v[2]), csub(v[0], v[2])
    r, t = cadd(v[1], v[3]), csub(v[1], v[3])
    t = rot(t, sign)
    return [cadd(p, r), cadd(q, t), csub(p, r), csub(q, t)]


def dft8(v, sign):
    e = dft4(v[0::2], sign)
    o = dft4(v[1::2], sign)
    a, b = o[1], o[3]
    if sign > 0:
        o[1] = (H * (a[0] - a[1]), H * (a[0] + a[1]))
        o[3] = (-H * (b[0] + b[1]), H * (b[0] - b[1]))
    else:
        o[1] = (H * (a[0] + a[1]), H * (a[1] - a[0]))
        o[3] = (H * (b[1] - b[0]), -H * (b[0] + b[1]))
    o[2] = rot(o[2], sign)
    return [cadd(e[i], o[i]) for i in range(4)] + [csub(e[i], o[i]) for i in range(4)]


def dft32(load, store, sign):
    mid = {}
    for n2 in range(4):
        out = dft8([load(4 * n1 + n2) for n1 in range(8)], sign)
        for k1 in range(8):
            v = out[k1]
            if n2 * k1 == 4:
                v = (H * (v[0] - sign * v[1]), H * (v[1] + sign * v[0]))
            elif n2 * k1:
                turn = sign * 2.0 * math.pi * n2 * k1 / 32
                c, s = math.cos(turn), math.sin(turn)
                v = (v[0] * c - v[1] * s, v[0] * s + v[1] * c)
            mid[n2, k1] = v
    for k1 in range(8):
        out = dft4([mid[n2, k1] for n2 in range(4)], sign)
        for k2 in range(4):
            store(k1 + 8 * k2, out[k2])


def split(x):
    hi = x.astype(BF)
    return hi, (x - hi.astype(F32)).astype(BF)


def dot(a, b):
    return jnp.dot(a, b, preferred_element_type=F32)


def forward_slabs(active, targ, phi, fz, tw, z, s):
    count = len(active)

    def pick(u, values):
        total, chosen, row = values[0], 1, list(values)
        for order in range(1, count):
            row = [after - before for before, after in zip(row, row[1:])]
            chosen = chosen * (u - order + 1)
            total = total + row[0] * (chosen // math.factorial(order))
        return total

    @pl.loop(0, count)
    def _(u):
        n = pick(u, [n for n, _ in active])
        slab = pick(u, [slab for _, slab in active])

        def load(y):
            at = slice(128 * y, 128 * (y + 1))
            t = targ[n, slab, :, at]
            return t * phi[0, slab, :, at], t * phi[1, slab, :, at]

        def store(k, v):
            c, w = tw[k, 0], tw[k, 1]
            s[u, k, :, 0:128] = v[0] * c + v[1] * w
            s[u, k, :, 128:256] = v[1] * c - v[0] * w

        dft32(load, store, -1)

    hi, lo = split(s[0:count].reshape(count * 256, 256))
    res = dot(jnp.concatenate([hi, lo, hi], 1), fz[...])
    for u, (n, slab) in enumerate(active):
        part = res[256 * u : 256 * (u + 1)]
        base = pl.multiple_of(8 * slab, 8)
        z[n, :, pl.ds(base, 8), :] = part[:, :128].reshape(32, 8, 128)
        z[n, :, pl.ds(64 + base, 8), :] = part[:, 128:].reshape(32, 8, 128)


def middle(n, kern, fx, ix, z):
    @pl.loop(0, 32 // YA)
    def _(step):
        ks = [step * YA + i for i in range(YA)]
        hi, lo = split(jnp.concatenate([z[n, k] for k in ks], 1))
        res = dot(fx[...], jnp.concatenate([hi, lo, hi], 0))
        kv = jnp.concatenate([kern[k] for k in ks], 1)
        hi, lo = split(res * jnp.concatenate([kv, kv], 0))
        res = dot(ix[...], jnp.concatenate([hi, lo, hi], 0))
        for i in range(YA):
            z[n, step * YA + i] = res[:, 128 * i : 128 * (i + 1)]


def inverse_slabs(n, parity, phi, iz, tw, z, s, part):
    rows = []
    for zz in range(4):
        base = pl.multiple_of(16 * zz + 8 * parity, 8)
        re = z[n, :, pl.ds(base, 8), :].reshape(256, 128)
        im = z[n, :, pl.ds(64 + base, 8), :].reshape(256, 128)
        rows.append(jnp.concatenate([re, im], 1))
    hi, lo = split(jnp.concatenate(rows, 0))
    s[0:4] = dot(jnp.concatenate([hi, lo, hi], 1), iz[...]).reshape(4, 32, 8, 256)

    @pl.loop(0, 4)
    def _(zz):
        slab = 2 * zz + parity

        def load(k):
            c, w = tw[k, 0], tw[k, 1]
            r, i = s[zz, k, :, 0:128], s[zz, k, :, 128:256]
            return r * c - i * w, i * c + r * w

        def store(y, v):
            at = slice(128 * y, 128 * (y + 1))
            part[zz, :, at] = v[0] * phi[0, slab, :, at] + v[1] * phi[1, slab, :, at]

        dft32(load, store, 1)


def unpack_kernel(kp, kern):
    low = lax.broadcasted_iota(jnp.int32, (64, 128), 1) < 64

    @pl.loop(0, 4)
    def _(slab):
        @pl.loop(0, 4)
        def _(r):
            a, b = kp[slab, r], kp[slab + 4, r]
            kern[slab * 8 + r] = jnp.where(low, a, pltpu.roll(b, 64, 1))
            kern[slab * 8 + 4 + r] = jnp.where(low, pltpu.roll(a, 64, 1), b)


def body(
    orb, kernel, fx_in, ix_in, fz_in, iz_in, tw_in, out,
    phi, targ, kslab, kpk, kp, kern, z, s, part, rcore, acc, extra, fx, ix, fz, iz, tw, send, recv, local,
):
    b = lax.axis_index("band")
    q = lax.axis_index("grid")

    def mod(value, n):
        return lax.rem(value, jnp.int32(n))

    def div(value, n):
        return lax.div(value, jnp.int32(n))

    core, block, x = mod(b, 2), div(b, 2), div(b, 4)
    plane, ylo = div(q, 2), mod(q, 2)
    odd = mod(ylo + block, 2)
    home = mod(core + block, 2)
    chip = block * 2 + odd
    sibling = (block * 2 + 1 - core, q)
    near = (b, plane * 2 + 1 - ylo)
    mine = core == odd
    owner = core == div(plane, 2)
    planes = [plane] + [mod(plane + d, 4) for d in (1, 2, 3)]
    parities = [ylo, 1 - ylo]
    slabs = [[2 * zz + p for p in parities] for zz in planes]
    targets_here = [div(zz, 2) == core for zz in planes]
    kt = mod(plane, 2)
    other = 1 - kt
    band_of = [kt, other, kt, other]
    across = [(b, 2 * zz + ylo) for zz in planes]
    near_slabs = [[2 * zz + mod(ylo + 1 - odd + i, 2) for i in range(2)] for zz in planes]

    def device(h, c, zz):
        h = mod(h + 16, 16)
        half = div(h, 2)
        return (half * 2 + c, zz * 2 + mod(h + half, 2))

    def at_plane(d):
        return across[d]

    def result_device(n, zz):
        return (mod(chip + n, 16), zz * 2 + home)

    count = [0]

    def slots(n):
        count[0] += n
        return count[0] - n

    def remote(src, dst, s, where, r=None):
        return pltpu.make_async_remote_copy(
            src_ref=src, dst_ref=dst, send_sem=send.at[s], recv_sem=recv.at[s if r is None else r],
            device_id=where, device_id_type=MESH,
        )

    sent, sent_owner = [], []

    def start(cp):
        cp.start()
        sent.append(cp)

    loads = [
        pltpu.make_async_copy(src, dst, local.at[i])
        for i, (src, dst) in enumerate(
            [(kernel, kslab), (fx_in, fx), (ix_in, ix), (fz_in, fz), (iz_in, iz), (tw_in, tw)]
        )
    ]
    for cp in loads:
        cp.start()

    barrier = pltpu.get_barrier_semaphore()
    greeted = []
    for dc in range(2):
        for dq in range(8):
            if dc or dq:
                greeted.append((mod(b + dc, 2) + block * 2, mod(q + dq, 8)))
    for dh in (-2, -1, 1, 2):
        greeted.append(device(chip + dh, core, plane))
    for n in (1, 2):
        behind = mod(b - n + 16, 16)
        behind_core = mod(ylo + div(behind, 2), 2)
        for zz in range(4):
            greeted.append(result_device(n, zz))
            greeted.append(device(behind, behind_core, zz))
    for dx in (4, 8, 12):
        greeted.append((mod(b + dx, 16), q))
    for where in greeted:
        pl.semaphore_signal(barrier, inc=1, device_id=where, device_id_type=MESH)
    pl.semaphore_wait(barrier, len(greeted))

    s_first = slots(4)
    firsts = {}
    for k in range(2):
        for dc in range(2):
            c = (core, 1 - core)[dc]
            src, dst = orb.at[2 * c + k], phi.at[k, q]
            firsts[dc, k] = remote(src, dst, s_first + 2 * dc + k, (block * 2 + c, plane * 2 + home), s_first + 2 * ylo + k)
    s_direct = slots(6)

    def direct(d):
        k = planes[d]
        slot = s_direct + 2 * d - 2
        return remote(orb.at[k], phi.at[band_of[d], q], slot, (block * 2 + div(k, 2), k * 2 + home), slot + ylo)

    def direct_wait(d, i):
        piece = phi.at[kt, slabs[d][i]]
        remote(piece, piece, s_direct, (b, q), s_direct + 2 * (4 - d) - 2 + parities[i]).wait_recv()

    for d in (1, 3, 2):
        start(direct(d))
    keeps = [pltpu.make_async_copy(orb.at[2 * core + k], phi.at[k, q], local.at[6 + k]) for k in range(2)]
    for k in range(2):

        @pl.when(mine)
        def _():
            keeps[k].start()

        @pl.when(jnp.logical_not(mine))
        def _():
            firsts[0, k].start()

        start(firsts[1, k])

    def wait_first(i):
        p = parities[i]
        for k in range(2):
            piece = phi.at[k, slabs[0][i]]
            cp = remote(piece, piece, s_first, (b, q), s_first + 2 * p + k)
            if i == 0:

                @pl.when(mine)
                def _():
                    keeps[k].wait()

                @pl.when(jnp.logical_not(mine))
                def _():
                    cp.wait_recv()
            else:
                cp.wait_recv()

    s_step = slots(8)
    s_pass = slots(4)

    def slab_at(d, i):
        return slabs[d][i]

    def step_copy(i, side, k):
        d = (1, 3)[side]
        piece = phi.at[k, slab_at(0, i)]
        return remote(piece, piece, s_step + 4 * i + 2 * side + k, at_plane(d))

    def start_it(cp):
        cp.start()

    def wait_sent(cp):
        cp.wait_send()

    def step_wait(i, side, k):
        piece = phi.at[k, slab_at((3, 1)[side], i)]
        remote(piece, piece, s_step, (b, q), s_step + 4 * i + 2 * side + k).wait_recv()

    def pass_copy(i, which):
        side = (i + which) % 2
        piece = phi.at[band_of[which], slab_at((3, 1)[side], i)]
        return remote(piece, piece, s_pass + 2 * i + which, at_plane((1, 3)[side]), s_pass + 2 * i + band_of[which])

    def pass_wait(i, k):
        piece = phi.at[k, slab_at(2, i)]
        remote(piece, piece, s_pass, (b, q), s_pass + 2 * i + k).wait_recv()

    def unless(condition):
        return pl.when(jnp.logical_not(condition))

    def each_other(i, act):
        for side, d in enumerate((1, 3)):
            act(step_copy(i, side, kt))

            @unless(targets_here[d])
            def _():
                act(step_copy(i, side, other))

    def each_pass(i, act):
        act(pass_copy(i, 0))

        @unless(targets_here[(3, 1)[i]])
        def _():
            act(pass_copy(i, 1))

    s_t0 = slots(8)
    s_t1 = slots(8)
    s_t2 = slots(8)
    s_t1_give = slots(8)
    s_t2_give = slots(8)
    order = [(0, 0), (3, 0), (1, 0), (0, 1), (2, 0), (1, 1), (3, 1), (2, 1)]
    far_back = device(chip - 2, core, plane)
    near_back = device(chip - 1, core, plane)

    def target_slab(n, j):
        d, i = order[j]
        return (slabs[d][i], near_slabs[d][i], slabs[d][1 - i])[n]

    def own_target(j):
        s = target_slab(0, j)
        src = phi.at[kt, s]
        keep = pltpu.make_async_copy(src, targ.at[0, s], local.at[8 + j])
        give = remote(src, targ.at[0, s], s_t0 + j, sibling)
        back = remote(src, targ.at[2, s], s_t2 + j, far_back)
        beside = remote(src, targ.at[1, s], s_t1 + j, near_back)
        return keep, give, back, beside

    def target_ready(j):
        @pl.when(owner)
        def _():
            keep, give, back, beside = own_target(j)
            back.start()
            if j in RELAYED:

                @pl.when(odd == 1)
                def _():
                    beside.start()
            else:
                beside.start()
            give.start()
            keep.start()

    def far_target(j):
        s = target_slab(2, j)
        piece = targ.at[2, s]
        arrive = remote(piece, piece, s_t2, (b, q), s_t2 + j)
        relay = remote(piece, targ.at[1, s], s_t1 + j, near)
        give = remote(piece, piece, s_t2_give + j, sibling)
        return arrive, relay, give

    def far_ready(j):
        @pl.when(owner)
        def _():
            arrive, relay, give = far_target(j)
            arrive.wait_recv()
            if j in RELAYED:

                @pl.when(odd == 0)
                def _():
                    relay.start()

            give.start()

    def near_target(j):
        piece = targ.at[1, target_slab(1, j)]
        return remote(piece, piece, s_t1, (b, q), s_t1 + j), remote(piece, piece, s_t1_give + j, sibling)

    def near_ready(j):
        @pl.when(owner)
        def _():
            arrive, give = near_target(j)
            arrive.wait_recv()
            give.start()

    def wait_target(n, j):
        base = (s_t0, s_t1_give, s_t2_give)[n]

        @pl.when(jnp.logical_not(owner))
        def _():
            piece = targ.at[n, target_slab(n, j)]
            remote(piece, piece, base, (b, q), base + j).wait_recv()

        if n == 0:

            @pl.when(owner)
            def _():
                own_target(j)[0].wait()

    s_kernel = slots(11)
    kx_half = pl.ds(pl.multiple_of(32 * core, 32), 32)
    kernel_first = [
        remote(kpk.at[x, kx_half], kp.at[q, x, kx_half], s_kernel + d - 1, (b, mod(q + d, 8))) for d in range(1, 8)
    ]
    kernel_second = [
        remote(kp.at[:, x, kx_half], kp.at[:, x, kx_half], s_kernel + 6 + d, (mod(b + 4 * d, 16), q)) for d in (1, 3, 2)
    ]
    kernel_third = remote(kp.at[:, :, kx_half], kp.at[:, :, kx_half], s_kernel + 10, sibling)

    def pack_kernel():
        for r in range(4):
            kpk[r] = jnp.concatenate([kslab[:, r, :], kslab[:, r + 4, :]], 1)
        for cp in kernel_first:
            start(cp)
        kp[q, x, kx_half] = kpk[x, kx_half]

    def forward(*active):
        for n, j in active:
            wait_target(n, j)
        forward_slabs([(n, target_slab(n, j)) for n, j in active], targ, phi, fz, tw, z, s)

    def near_others(i, side):
        step_wait(i, side, other)

        @unless(owner)
        def _():
            step_wait(i, side, kt)

    def far_others(i):
        pass_wait(i, other)

        @unless(owner)
        def _():
            pass_wait(i, kt)

    def target_here(j):
        @pl.when(owner)
        def _():
            direct_wait(*order[j])

        target_ready(j)

    wait_first(0)
    each_other(0, start_it)
    target_ready(0)
    target_here(1)
    target_here(2)
    loads[0].wait()
    pack_kernel()
    target_here(4)
    target_here(5)
    target_here(6)
    for cp in loads[1:]:
        cp.wait()
    forward((0, 0))
    near_others(0, 0)
    near_others(0, 1)
    each_pass(0, start_it)
    target_here(7)
    wait_first(1)
    each_other(1, start_it)
    target_ready(3)
    far_ready(0)
    forward((0, 1), (0, 2))
    for j in (1, 2, 5, 6, 4):
        far_ready(j)
    forward((0, 3))
    for cp in kernel_first:
        cp.wait_recv()
    for cp in kernel_second:
        start(cp)
    far_ready(7)
    near_others(1, 1)
    near_others(1, 0)
    each_pass(1, start_it)
    far_ready(3)
    far_others(0)
    forward((0, 4), (2, 5), (2, 6), (2, 3))
    for cp in kernel_second:
        cp.wait_recv()
    start(kernel_third)
    forward((0, 5), (0, 6), (2, 7))
    kernel_third.wait_recv()
    unpack_kernel(kp, kern)
    far_others(1)
    forward((0, 7))

    s_core = slots(3)
    s_result = slots(12)

    def core_sum(n):
        return remote(part.at[n, 0], rcore.at[n], s_core + n, sibling)

    def result(n, d):
        zz = planes[d]
        return remote(part.at[n, 1, zz], acc.at[n, plane], s_result + 4 * n + d, result_device(n, zz))

    s_extra = slots(4)
    adds = jnp.logical_and(odd == 0, core == 1)
    gives = jnp.logical_and(odd == 1, core == 1)
    has_near = jnp.logical_or(odd == 1, core == 1)

    def exchange(d):
        return remote(part.at[1, 1, planes[d]], extra.at[planes[d]], s_extra + d, near)

    result_keep = pltpu.make_async_copy(part.at[0, 1, plane], acc.at[0, plane], local.at[16])

    def finish(n):
        core_sum(n).wait_recv()

        @pl.loop(0, 4)
        def _(i):
            part[n, 1, i] = part[n, 1, i] + rcore[n, i]

        held = jnp.logical_or(jnp.logical_and(adds, n == 2), jnp.logical_and(gives, n == 1))

        @unless(held)
        def _():
            for d in (2, 1, 3):
                result(n, d).start()

        @unless(jnp.logical_or(held, jnp.logical_and(n == 0, mine)))
        def _():
            result(n, 0).start()

        @pl.when(jnp.logical_and(gives, n == 1))
        def _():
            for d in (2, 1, 3, 0):
                exchange(d).start()

    @pl.loop(0, 3)
    def _(u):
        n = mod(2 * u, 3)

        @pl.when(u == 1)
        def _():
            for j in range(8):
                near_ready(j)
            forward((2, 0), (2, 1), (2, 2), (2, 4))

        @pl.when(u == 2)
        def _():
            for j in (0, 4):
                forward((1, j), (1, j + 1), (1, j + 2), (1, j + 3))

        middle(n, kern, fx, ix, z)

        last = div(u, 2)

        @pl.loop(0, 2)
        def _(g):
            place = mod(g + core * last, 2)
            inverse_slabs(n, mod(home + 1 + g + core * last, 2), phi, iz, tw, z, s, part.at[n, place])

            @pl.when(place == 0)
            def _():
                core_sum(n).start()

            @pl.when(place == 1)
            def _():
                finish(n)

    @pl.when(adds)
    def _():
        for d in (2, 1, 3, 0):
            exchange(d).wait_recv()
            part[2, 1, planes[d]] = part[2, 1, planes[d]] + extra[planes[d]]
            result(2, d).start()

    @pl.when(mine)
    def _():
        result_keep.start()
        result_keep.wait()

    for n in range(3):
        core_sum(n).wait_send()
    for d in range(4):
        result(2, d).wait()
        if d:
            result(0, d).wait()

    @unless(mine)
    def _():
        result(0, 0).wait()

    @pl.when(gives)
    def _():
        for d in range(4):
            exchange(d).wait_send()

    @unless(gives)
    def _():
        for d in range(4):
            result(1, d).wait_send()

    @pl.when(has_near)
    def _():
        for d in range(4):
            result(1, d).wait_recv()

        @pl.loop(0, 4)
        def _(i):
            out[i] = acc[0, i] + acc[1, i] + acc[2, i]

    @unless(has_near)
    def _():
        @pl.loop(0, 4)
        def _(i):
            out[i] = acc[0, i] + acc[2, i]

    for cp in sent:
        cp.wait_send()
    for i in range(2):
        each_other(i, wait_sent)
        each_pass(i, wait_sent)

    @pl.when(jnp.logical_not(mine))
    def _():
        for k in range(2):
            firsts[0, k].wait_send()

    @pl.when(owner)
    def _():
        for j in range(8):
            keep, give, back, beside = own_target(j)
            give.wait_send()
            back.wait_send()
            arrive, relay, pass_on = far_target(j)
            pass_on.wait_send()
            if j in RELAYED:

                @pl.when(odd == 1)
                def _():
                    beside.wait_send()

                @pl.when(odd == 0)
                def _():
                    relay.wait_send()
            else:
                beside.wait_send()
            near_target(j)[1].wait_send()


def local(orbitals, kernel):
    vmem = pl.BlockSpec(memory_space=pltpu.VMEM)
    anywhere = pl.BlockSpec(memory_space=pl.ANY)
    constants = [jnp.asarray(table) for table in tables()]
    return pl.pallas_call(
        body,
        out_shape=pltpu.VMEM(orbitals.shape, F32),
        in_specs=[anywhere] * 7,
        out_specs=vmem,
        scratch_shapes=[
            pltpu.VMEM((2, 8, 8, 4096), F32),
            pltpu.VMEM((3, 8, 8, 4096), F32),
            pltpu.VMEM((64, 8, 64), F32),
            pltpu.VMEM((4, 64, 128), F32),
            pltpu.VMEM((8, 4, 64, 128), F32),
            pltpu.VMEM((32, 64, 128), F32),
            pltpu.VMEM((3, 32, 128, 128), F32),
            pltpu.VMEM((5, 32, 8, 256), F32),
            pltpu.VMEM((3, 2, 4, 8, 4096), F32),
            pltpu.VMEM((3, 4, 8, 4096), F32),
            pltpu.VMEM((3, 4, 8, 4096), F32),
            pltpu.VMEM((4, 8, 4096), F32),
        ]
        + [pltpu.VMEM(table.shape, table.dtype) for table in constants]
        + [
            pltpu.SemaphoreType.DMA((92,)),
            pltpu.SemaphoreType.DMA((92,)),
            pltpu.SemaphoreType.DMA((17,)),
        ],
        compiler_params=pltpu.CompilerParams(
            collective_id=0, has_side_effects=True, vmem_limit_bytes=56 * 2**20
        ),
    )(orbitals, kernel, *constants)


def solution(mesh):
    return jax.shard_map(
        local,
        mesh=mesh,
        in_specs=(P("band", "grid", None), P(None, "grid", None)),
        out_specs=P("band", "grid", None),
        check_vma=False,
    )
```

```python
import math

import jax
import jax.numpy as jnp
import ml_dtypes
import numpy as np
from jax import lax
from jax.experimental import pallas as pl
from jax.experimental.pallas import tpu as pltpu
from jax.sharding import PartitionSpec as P

G = 64
BF = jnp.bfloat16
F32 = jnp.float32
H = math.sqrt(0.5)
MESH = pl.DeviceIdType.MESH
YA = 32
RELAYED = (0, 1, 2, 3, 4, 5, 6, 7)


def split_table(matrix):
    hi = matrix.astype(ml_dtypes.bfloat16)
    return hi, (matrix - hi.astype(np.float64)).astype(ml_dtypes.bfloat16)


def tables():
    k = np.arange(G)
    angle = 2.0 * np.pi * ((k[:, None] * k[None, :]) % G) / G
    c, s = np.cos(angle), np.sin(angle)

    def left(matrix):
        hi, lo = split_table(matrix)
        return np.concatenate([hi, hi, lo], 1)

    def right(matrix):
        hi, lo = split_table(matrix)
        return np.concatenate([hi, hi, lo], 0)

    forward_x = left(np.block([[c, s], [-s, c]]))
    inverse_x = left(np.block([[c, -s], [s, c]]))
    parity = np.array([[1.0, 1.0], [1.0, -1.0]])
    cc, ss = np.kron(parity, c), np.kron(parity, s)
    forward_z = right(np.block([[cc, -ss], [ss, cc]]))
    inverse_z = right(np.block([[cc, ss], [-ss, cc]]) * (-1.0 / G**3))
    twiddle = np.ones((32, 2, 8, 128), np.float64)
    turn = 2.0 * np.pi * np.arange(32) / G
    twiddle[:, 0, :, 64:] = np.cos(turn)[:, None, None]
    twiddle[:, 1, :, :64] = 0.0
    twiddle[:, 1, :, 64:] = np.sin(turn)[:, None, None]
    return forward_x, inverse_x, forward_z, inverse_z, twiddle.astype(np.float32)


def cadd(a, b):
    return a[0] + b[0], a[1] + b[1]


def csub(a, b):
    return a[0] - b[0], a[1] - b[1]


def rot(a, sign):
    return (-a[1], a[0]) if sign > 0 else (a[1], -a[0])


def dft4(v, sign):
    p, q = cadd(v[0], v[2]), csub(v[0], v[2])
    r, t = cadd(v[1], v[3]), csub(v[1], v[3])
    t = rot(t, sign)
    return [cadd(p, r), cadd(q, t), csub(p, r), csub(q, t)]


def dft8(v, sign):
    e = dft4(v[0::2], sign)
    o = dft4(v[1::2], sign)
    a, b = o[1], o[3]
    if sign > 0:
        o[1] = (H * (a[0] - a[1]), H * (a[0] + a[1]))
        o[3] = (-H * (b[0] + b[1]), H * (b[0] - b[1]))
    else:
        o[1] = (H * (a[0] + a[1]), H * (a[1] - a[0]))
        o[3] = (H * (b[1] - b[0]), -H * (b[0] + b[1]))
    o[2] = rot(o[2], sign)
    return [cadd(e[i], o[i]) for i in range(4)] + [csub(e[i], o[i]) for i in range(4)]


def dft32(load, store, sign):
    mid = {}
    for n2 in range(4):
        out = dft8([load(4 * n1 + n2) for n1 in range(8)], sign)
        for k1 in range(8):
            v = out[k1]
            if n2 * k1 == 4:
                v = (H * (v[0] - sign * v[1]), H * (v[1] + sign * v[0]))
            elif n2 * k1:
                turn = sign * 2.0 * math.pi * n2 * k1 / 32
                c, s = math.cos(turn), math.sin(turn)
                v = (v[0] * c - v[1] * s, v[0] * s + v[1] * c)
            mid[n2, k1] = v
    for k1 in range(8):
        out = dft4([mid[n2, k1] for n2 in range(4)], sign)
        for k2 in range(4):
            store(k1 + 8 * k2, out[k2])


def split(x):
    hi = x.astype(BF)
    return hi, (x - hi.astype(F32)).astype(BF)


def dot(a, b):
    return jnp.dot(a, b, preferred_element_type=F32)


def forward_slabs(active, targ, phi, fz, tw, z, s, apart=False):
    count = len(active)

    def pick(u, values):
        total, chosen, row = values[0], 1, list(values)
        for order in range(1, count):
            row = [after - before for before, after in zip(row, row[1:])]
            chosen = chosen * (u - order + 1)
            total = total + row[0] * (chosen // math.factorial(order))
        return total

    def transform(u, n, slab):
        def load(y):
            at = slice(128 * y, 128 * (y + 1))
            t = targ[n, slab, :, at]
            return t * phi[0, slab, :, at], t * phi[1, slab, :, at]

        def store(k, v):
            c, w = tw[k, 0], tw[k, 1]
            s[u, k, :, 0:128] = v[0] * c + v[1] * w
            s[u, k, :, 128:256] = v[1] * c - v[0] * w

        dft32(load, store, -1)

    def multiply(first, last):
        hi, lo = split(s[first:last].reshape((last - first) * 256, 256))
        res = dot(jnp.concatenate([hi, lo, hi], 1), fz[...])
        for u, (n, slab) in enumerate(active[first:last]):
            part = res[256 * u : 256 * (u + 1)]
            base = pl.multiple_of(8 * slab, 8)
            z[n, :, pl.ds(base, 8), :] = part[:, :128].reshape(32, 8, 128)
            z[n, :, pl.ds(64 + base, 8), :] = part[:, 128:].reshape(32, 8, 128)

    if apart:
        for u, (n, slab) in enumerate(active):
            transform(u, n, slab)
            if u % 2 or u == count - 1:
                multiply(u - u % 2, u + 1)
    else:

        @pl.loop(0, count)
        def _(u):
            transform(u, pick(u, [n for n, _ in active]), pick(u, [slab for _, slab in active]))

        multiply(0, count)


def middle(n, kern, fx, ix, z):
    @pl.loop(0, 32 // YA)
    def _(step):
        ks = [step * YA + i for i in range(YA)]
        hi, lo = split(jnp.concatenate([z[n, k] for k in ks], 1))
        res = dot(fx[...], jnp.concatenate([hi, lo, hi], 0))
        kv = jnp.concatenate([kern[k] for k in ks], 1)
        hi, lo = split(res * jnp.concatenate([kv, kv], 0))
        res = dot(ix[...], jnp.concatenate([hi, lo, hi], 0))
        for i in range(YA):
            z[n, step * YA + i] = res[:, 128 * i : 128 * (i + 1)]


def inverse_slabs(n, parity, phi, iz, tw, z, s, part):
    rows = []
    for zz in range(4):
        base = pl.multiple_of(16 * zz + 8 * parity, 8)
        re = z[n, :, pl.ds(base, 8), :].reshape(256, 128)
        im = z[n, :, pl.ds(64 + base, 8), :].reshape(256, 128)
        rows.append(jnp.concatenate([re, im], 1))
    hi, lo = split(jnp.concatenate(rows, 0))
    res = dot(jnp.concatenate([hi, lo, hi], 1), iz[...]).reshape(4, 32, 8, 256)
    for zz in range(4):
        slab = 2 * zz + parity

        def load(k):
            c, w = tw[k, 0], tw[k, 1]
            r, i = res[zz, k, :, 0:128], res[zz, k, :, 128:256]
            return r * c - i * w, i * c + r * w

        def store(y, v):
            at = slice(128 * y, 128 * (y + 1))
            part[zz, :, at] = v[0] * phi[0, slab, :, at] + v[1] * phi[1, slab, :, at]

        dft32(load, store, 1)


def unpack_kernel(kp, kern):
    low = lax.broadcasted_iota(jnp.int32, (64, 128), 1) < 64

    @pl.loop(0, 4)
    def _(slab):
        @pl.loop(0, 4)
        def _(r):
            a, b = kp[slab, r], kp[slab + 4, r]
            kern[slab * 8 + r] = jnp.where(low, a, pltpu.roll(b, 64, 1))
            kern[slab * 8 + 4 + r] = jnp.where(low, pltpu.roll(a, 64, 1), b)


def body(
    orb, kernel, fx_in, ix_in, fz_in, iz_in, tw_in, out,
    phi, targ, kslab, kpk, kp, kern, z, s, part, rcore, acc, extra, fx, ix, fz, iz, tw, send, recv, local,
):
    b = lax.axis_index("band")
    q = lax.axis_index("grid")

    def mod(value, n):
        return lax.rem(value, jnp.int32(n))

    def div(value, n):
        return lax.div(value, jnp.int32(n))

    core, block, x = mod(b, 2), div(b, 2), div(b, 4)
    plane, ylo = div(q, 2), mod(q, 2)
    odd = mod(ylo + block, 2)
    home = mod(core + block, 2)
    chip = block * 2 + odd
    sibling = (block * 2 + 1 - core, q)
    near = (b, plane * 2 + 1 - ylo)
    mine = core == odd
    owner = core == div(plane, 2)
    planes = [plane] + [mod(plane + d, 4) for d in (1, 2, 3)]
    parities = [ylo, 1 - ylo]
    slabs = [[2 * zz + p for p in parities] for zz in planes]
    targets_here = [div(zz, 2) == core for zz in planes]
    kt = mod(plane, 2)
    other = 1 - kt
    band_of = [kt, other, kt, other]
    across = [(b, 2 * zz + ylo) for zz in planes]
    near_slabs = [[2 * zz + mod(ylo + 1 - odd + i, 2) for i in range(2)] for zz in planes]

    def device(h, c, zz):
        h = mod(h + 16, 16)
        half = div(h, 2)
        return (half * 2 + c, zz * 2 + mod(h + half, 2))

    def at_plane(d):
        return across[d]

    def result_device(n, zz):
        return (mod(chip + n, 16), zz * 2 + home)

    count = [0]

    def slots(n):
        count[0] += n
        return count[0] - n

    def remote(src, dst, s, where, r=None):
        return pltpu.make_async_remote_copy(
            src_ref=src, dst_ref=dst, send_sem=send.at[s], recv_sem=recv.at[s if r is None else r],
            device_id=where, device_id_type=MESH,
        )

    sent, sent_owner = [], []

    def start(cp):
        cp.start()
        sent.append(cp)

    loads = [
        pltpu.make_async_copy(src, dst, local.at[i])
        for i, (src, dst) in enumerate(
            [(kernel, kslab), (fx_in, fx), (ix_in, ix), (fz_in, fz), (iz_in, iz), (tw_in, tw)]
        )
    ]
    for cp in loads:
        cp.start()

    barrier = pltpu.get_barrier_semaphore()
    greeted = []
    for dc in range(2):
        for dq in range(8):
            if dc or dq:
                greeted.append((mod(b + dc, 2) + block * 2, mod(q + dq, 8)))
    for dh in (-2, -1, 1, 2):
        greeted.append(device(chip + dh, core, plane))
    for n in (1, 2):
        behind = mod(b - n + 16, 16)
        behind_core = mod(ylo + div(behind, 2), 2)
        for zz in range(4):
            greeted.append(result_device(n, zz))
            greeted.append(device(behind, behind_core, zz))
    for dx in (4, 8, 12):
        greeted.append((mod(b + dx, 16), q))
    for where in greeted:
        pl.semaphore_signal(barrier, inc=1, device_id=where, device_id_type=MESH)
    pl.semaphore_wait(barrier, len(greeted))

    s_first = slots(4)
    firsts = {}
    for k in range(2):
        for dc in range(2):
            c = (core, 1 - core)[dc]
            src, dst = orb.at[2 * c + k], phi.at[k, q]
            firsts[dc, k] = remote(src, dst, s_first + 2 * dc + k, (block * 2 + c, plane * 2 + home), s_first + 2 * ylo + k)
    s_direct = slots(6)

    def direct(d):
        k = planes[d]
        slot = s_direct + 2 * d - 2
        return remote(orb.at[k], phi.at[band_of[d], q], slot, (block * 2 + div(k, 2), k * 2 + home), slot + ylo)

    def direct_wait(d, i):
        piece = phi.at[kt, slabs[d][i]]
        remote(piece, piece, s_direct, (b, q), s_direct + 2 * (4 - d) - 2 + parities[i]).wait_recv()

    for d in (1, 3, 2):
        start(direct(d))
    keeps = [pltpu.make_async_copy(orb.at[2 * core + k], phi.at[k, q], local.at[6 + k]) for k in range(2)]
    for k in range(2):

        @pl.when(mine)
        def _():
            keeps[k].start()

        @pl.when(jnp.logical_not(mine))
        def _():
            firsts[0, k].start()

        start(firsts[1, k])

    def wait_first(i):
        p = parities[i]
        for k in range(2):
            piece = phi.at[k, slabs[0][i]]
            cp = remote(piece, piece, s_first, (b, q), s_first + 2 * p + k)
            if i == 0:

                @pl.when(mine)
                def _():
                    keeps[k].wait()

                @pl.when(jnp.logical_not(mine))
                def _():
                    cp.wait_recv()
            else:
                cp.wait_recv()

    s_step = slots(8)
    s_pass = slots(4)

    def slab_at(d, i):
        return slabs[d][i]

    def step_copy(i, side, k):
        d = (1, 3)[side]
        piece = phi.at[k, slab_at(0, i)]
        return remote(piece, piece, s_step + 4 * i + 2 * side + k, at_plane(d))

    def start_it(cp):
        cp.start()

    def wait_sent(cp):
        cp.wait_send()

    def step_wait(i, side, k):
        piece = phi.at[k, slab_at((3, 1)[side], i)]
        remote(piece, piece, s_step, (b, q), s_step + 4 * i + 2 * side + k).wait_recv()

    def pass_copy(i, which):
        side = (i + which) % 2
        piece = phi.at[band_of[which], slab_at((3, 1)[side], i)]
        return remote(piece, piece, s_pass + 2 * i + which, at_plane((1, 3)[side]), s_pass + 2 * i + band_of[which])

    def pass_wait(i, k):
        piece = phi.at[k, slab_at(2, i)]
        remote(piece, piece, s_pass, (b, q), s_pass + 2 * i + k).wait_recv()

    def unless(condition):
        return pl.when(jnp.logical_not(condition))

    def each_other(i, act):
        for side, d in enumerate((1, 3)):
            act(step_copy(i, side, kt))

            @unless(targets_here[d])
            def _():
                act(step_copy(i, side, other))

    def each_pass(i, act):
        act(pass_copy(i, 0))

        @unless(targets_here[(3, 1)[i]])
        def _():
            act(pass_copy(i, 1))

    s_t0 = slots(8)
    s_t1 = slots(8)
    s_t2 = slots(8)
    s_t1_give = slots(8)
    s_t2_give = slots(8)
    order = [(0, 0), (3, 0), (1, 0), (0, 1), (2, 0), (1, 1), (3, 1), (2, 1)]
    far_back = device(chip - 2, core, plane)
    near_back = device(chip - 1, core, plane)

    def target_slab(n, j):
        d, i = order[j]
        return (slabs[d][i], near_slabs[d][i], slabs[d][1 - i])[n]

    def own_target(j):
        s = target_slab(0, j)
        src = phi.at[kt, s]
        keep = pltpu.make_async_copy(src, targ.at[0, s], local.at[8 + j])
        give = remote(src, targ.at[0, s], s_t0 + j, sibling)
        back = remote(src, targ.at[2, s], s_t2 + j, far_back)
        beside = remote(src, targ.at[1, s], s_t1 + j, near_back)
        return keep, give, back, beside

    def target_ready(j):
        @pl.when(owner)
        def _():
            keep, give, back, beside = own_target(j)
            back.start()
            if j in RELAYED:

                @pl.when(odd == 1)
                def _():
                    beside.start()
            else:
                beside.start()
            give.start()
            keep.start()

    def far_target(j):
        s = target_slab(2, j)
        piece = targ.at[2, s]
        arrive = remote(piece, piece, s_t2, (b, q), s_t2 + j)
        relay = remote(piece, targ.at[1, s], s_t1 + j, near)
        give = remote(piece, piece, s_t2_give + j, sibling)
        return arrive, relay, give

    def far_ready(j):
        @pl.when(owner)
        def _():
            arrive, relay, give = far_target(j)
            arrive.wait_recv()
            if j in RELAYED:

                @pl.when(odd == 0)
                def _():
                    relay.start()

            give.start()

    def near_target(j):
        piece = targ.at[1, target_slab(1, j)]
        return remote(piece, piece, s_t1, (b, q), s_t1 + j), remote(piece, piece, s_t1_give + j, sibling)

    def near_ready(j):
        @pl.when(owner)
        def _():
            arrive, give = near_target(j)
            arrive.wait_recv()
            give.start()

    def wait_target(n, j):
        base = (s_t0, s_t1_give, s_t2_give)[n]

        @pl.when(jnp.logical_not(owner))
        def _():
            piece = targ.at[n, target_slab(n, j)]
            remote(piece, piece, base, (b, q), base + j).wait_recv()

        if n == 0:

            @pl.when(owner)
            def _():
                own_target(j)[0].wait()

    s_kernel = slots(11)
    kx_half = pl.ds(pl.multiple_of(32 * core, 32), 32)
    kernel_first = [
        remote(kpk.at[x, kx_half], kp.at[q, x, kx_half], s_kernel + d - 1, (b, mod(q + d, 8))) for d in range(1, 8)
    ]
    kernel_second = [
        remote(kp.at[:, x, kx_half], kp.at[:, x, kx_half], s_kernel + 6 + d, (mod(b + 4 * d, 16), q)) for d in (1, 3, 2)
    ]
    kernel_third = remote(kp.at[:, :, kx_half], kp.at[:, :, kx_half], s_kernel + 10, sibling)

    def pack_kernel():
        for r in range(4):
            kpk[r] = jnp.concatenate([kslab[:, r, :], kslab[:, r + 4, :]], 1)
        for cp in kernel_first:
            start(cp)
        kp[q, x, kx_half] = kpk[x, kx_half]

    def forward(*active, apart=False):
        for n, j in active:
            wait_target(n, j)
        forward_slabs([(n, target_slab(n, j)) for n, j in active], targ, phi, fz, tw, z, s, apart)

    def near_others(i, side):
        step_wait(i, side, other)

        @unless(owner)
        def _():
            step_wait(i, side, kt)

    def far_others(i):
        pass_wait(i, other)

        @unless(owner)
        def _():
            pass_wait(i, kt)

    def target_here(j):
        @pl.when(owner)
        def _():
            direct_wait(*order[j])

        target_ready(j)

    wait_first(0)
    target_ready(0)
    each_other(0, start_it)
    target_here(1)
    target_here(2)
    loads[0].wait()
    pack_kernel()
    target_here(4)
    target_here(5)
    target_here(6)
    for cp in loads[1:]:
        cp.wait()
    forward((0, 0))
    near_others(0, 0)
    near_others(0, 1)
    each_pass(0, start_it)
    target_here(7)
    wait_first(1)
    target_ready(3)
    each_other(1, start_it)
    far_ready(0)
    forward((0, 1), (0, 2))
    for j in (1, 2, 5, 6, 4):
        far_ready(j)
    forward((0, 3))
    for cp in kernel_first:
        cp.wait_recv()
    for cp in kernel_second:
        start(cp)
    far_ready(7)
    near_others(1, 1)
    near_others(1, 0)
    each_pass(1, start_it)
    far_ready(3)
    far_others(0)
    forward((0, 4), (2, 5), (2, 6), (2, 3))
    for cp in kernel_second:
        cp.wait_recv()
    start(kernel_third)
    forward((0, 5), (0, 6), (2, 7))
    kernel_third.wait_recv()
    unpack_kernel(kp, kern)
    far_others(1)
    forward((0, 7))

    s_core = slots(3)
    s_result = slots(12)

    def core_sum(n):
        return remote(part.at[n, 0], rcore.at[n], s_core + n, sibling)

    def result(n, d):
        zz = planes[d]
        return remote(part.at[n, 1, zz], acc.at[n, plane], s_result + 4 * n + d, result_device(n, zz))

    s_extra = slots(4)
    adds = jnp.logical_and(odd == 0, core == 1)
    gives = jnp.logical_and(odd == 1, core == 1)
    has_near = jnp.logical_or(odd == 1, core == 1)

    def exchange(d):
        return remote(part.at[1, 1, planes[d]], extra.at[planes[d]], s_extra + d, near)

    result_keep = pltpu.make_async_copy(part.at[0, 1, plane], acc.at[0, plane], local.at[16])

    def finish(n):
        core_sum(n).wait_recv()

        @pl.loop(0, 4)
        def _(i):
            part[n, 1, i] = part[n, 1, i] + rcore[n, i]

        held = jnp.logical_or(jnp.logical_and(adds, n == 2), jnp.logical_and(gives, n == 1))

        @unless(held)
        def _():
            for d in (2, 1, 3):
                result(n, d).start()

        @unless(jnp.logical_or(held, jnp.logical_and(n == 0, mine)))
        def _():
            result(n, 0).start()

        @pl.when(jnp.logical_and(gives, n == 1))
        def _():
            for d in (2, 1, 3, 0):
                exchange(d).start()

    @pl.loop(0, 3)
    def _(u):
        n = mod(2 * u, 3)

        @pl.when(u == 1)
        def _():
            for j in range(8):
                near_ready(j)
            forward((2, 0), (2, 1), (2, 2), (2, 4), apart=True)

        @pl.when(u == 2)
        def _():
            for j in (0, 4):
                forward((1, j), (1, j + 1), (1, j + 2), (1, j + 3), apart=True)

        middle(n, kern, fx, ix, z)

        last = div(u, 2)

        @pl.loop(0, 2)
        def _(g):
            place = mod(g + core * last, 2)
            inverse_slabs(n, mod(home + 1 + g + core * last, 2), phi, iz, tw, z, s, part.at[n, place])

            @pl.when(place == 0)
            def _():
                core_sum(n).start()

            @pl.when(place == 1)
            def _():
                finish(n)

    @pl.when(adds)
    def _():
        for d in (2, 1, 3, 0):
            exchange(d).wait_recv()
            part[2, 1, planes[d]] = part[2, 1, planes[d]] + extra[planes[d]]
            result(2, d).start()

    @pl.when(mine)
    def _():
        result_keep.start()
        result_keep.wait()

    for n in range(3):
        core_sum(n).wait_send()
    for d in range(4):
        result(2, d).wait()
        if d:
            result(0, d).wait()

    @unless(mine)
    def _():
        result(0, 0).wait()

    @pl.when(gives)
    def _():
        for d in range(4):
            exchange(d).wait_send()

    @unless(gives)
    def _():
        for d in range(4):
            result(1, d).wait_send()

    @pl.when(has_near)
    def _():
        for d in range(4):
            result(1, d).wait_recv()

        @pl.loop(0, 4)
        def _(i):
            out[i] = acc[0, i] + acc[1, i] + acc[2, i]

    @unless(has_near)
    def _():
        @pl.loop(0, 4)
        def _(i):
            out[i] = acc[0, i] + acc[2, i]

    for cp in sent:
        cp.wait_send()
    for i in range(2):
        each_other(i, wait_sent)
        each_pass(i, wait_sent)

    @pl.when(jnp.logical_not(mine))
    def _():
        for k in range(2):
            firsts[0, k].wait_send()

    @pl.when(owner)
    def _():
        for j in range(8):
            keep, give, back, beside = own_target(j)
            give.wait_send()
            back.wait_send()
            arrive, relay, pass_on = far_target(j)
            pass_on.wait_send()
            if j in RELAYED:

                @pl.when(odd == 1)
                def _():
                    beside.wait_send()

                @pl.when(odd == 0)
                def _():
                    relay.wait_send()
            else:
                beside.wait_send()
            near_target(j)[1].wait_send()


def local(orbitals, kernel):
    vmem = pl.BlockSpec(memory_space=pltpu.VMEM)
    anywhere = pl.BlockSpec(memory_space=pl.ANY)
    constants = [jnp.asarray(table) for table in tables()]
    return pl.pallas_call(
        body,
        out_shape=pltpu.VMEM(orbitals.shape, F32),
        in_specs=[anywhere] * 7,
        out_specs=vmem,
        scratch_shapes=[
            pltpu.VMEM((2, 8, 8, 4096), F32),
            pltpu.VMEM((3, 8, 8, 4096), F32),
            pltpu.VMEM((64, 8, 64), F32),
            pltpu.VMEM((4, 64, 128), F32),
            pltpu.VMEM((8, 4, 64, 128), F32),
            pltpu.VMEM((32, 64, 128), F32),
            pltpu.VMEM((3, 32, 128, 128), F32),
            pltpu.VMEM((5, 32, 8, 256), F32),
            pltpu.VMEM((3, 2, 4, 8, 4096), F32),
            pltpu.VMEM((3, 4, 8, 4096), F32),
            pltpu.VMEM((3, 4, 8, 4096), F32),
            pltpu.VMEM((4, 8, 4096), F32),
        ]
        + [pltpu.VMEM(table.shape, table.dtype) for table in constants]
        + [
            pltpu.SemaphoreType.DMA((92,)),
            pltpu.SemaphoreType.DMA((92,)),
            pltpu.SemaphoreType.DMA((17,)),
        ],
        compiler_params=pltpu.CompilerParams(
            collective_id=0, has_side_effects=True, vmem_limit_bytes=56 * 2**20
        ),
    )(orbitals, kernel, *constants)


def solution(mesh):
    return jax.shard_map(
        local,
        mesh=mesh,
        in_specs=(P("band", "grid", None), P(None, "grid", None)),
        out_specs=P("band", "grid", None),
        check_vma=False,
    )
```

```python
import math

import jax
import jax.numpy as jnp
import ml_dtypes
import numpy as np
from jax import lax
from jax.experimental import pallas as pl
from jax.experimental.pallas import tpu as pltpu
from jax.sharding import PartitionSpec as P

G = 64
BF = jnp.bfloat16
F32 = jnp.float32
H = math.sqrt(0.5)
MESH = pl.DeviceIdType.MESH
YA = 32
RELAYED = (0, 1, 2, 3, 4, 5, 6, 7)


def split_table(matrix):
    hi = matrix.astype(ml_dtypes.bfloat16)
    return hi, (matrix - hi.astype(np.float64)).astype(ml_dtypes.bfloat16)


def tables():
    k = np.arange(G)
    angle = 2.0 * np.pi * ((k[:, None] * k[None, :]) % G) / G
    c, s = np.cos(angle), np.sin(angle)

    def left(matrix):
        hi, lo = split_table(matrix)
        return np.concatenate([hi, hi, lo], 1)

    def right(matrix):
        hi, lo = split_table(matrix)
        return np.concatenate([hi, hi, lo], 0)

    forward_x = left(np.block([[c, s], [-s, c]]))
    inverse_x = left(np.block([[c, -s], [s, c]]))
    parity = np.array([[1.0, 1.0], [1.0, -1.0]])
    cc, ss = np.kron(parity, c), np.kron(parity, s)
    forward_z = right(np.block([[cc, -ss], [ss, cc]]))
    inverse_z = right(np.block([[cc, ss], [-ss, cc]]) * (-1.0 / G**3))
    twiddle = np.ones((32, 2, 8, 128), np.float64)
    turn = 2.0 * np.pi * np.arange(32) / G
    twiddle[:, 0, :, 64:] = np.cos(turn)[:, None, None]
    twiddle[:, 1, :, :64] = 0.0
    twiddle[:, 1, :, 64:] = np.sin(turn)[:, None, None]
    return forward_x, inverse_x, forward_z, inverse_z, twiddle.astype(np.float32)


def cadd(a, b):
    return a[0] + b[0], a[1] + b[1]


def csub(a, b):
    return a[0] - b[0], a[1] - b[1]


def rot(a, sign):
    return (-a[1], a[0]) if sign > 0 else (a[1], -a[0])


def dft4(v, sign):
    p, q = cadd(v[0], v[2]), csub(v[0], v[2])
    r, t = cadd(v[1], v[3]), csub(v[1], v[3])
    t = rot(t, sign)
    return [cadd(p, r), cadd(q, t), csub(p, r), csub(q, t)]


def dft8(v, sign):
    e = dft4(v[0::2], sign)
    o = dft4(v[1::2], sign)
    a, b = o[1], o[3]
    if sign > 0:
        o[1] = (H * (a[0] - a[1]), H * (a[0] + a[1]))
        o[3] = (-H * (b[0] + b[1]), H * (b[0] - b[1]))
    else:
        o[1] = (H * (a[0] + a[1]), H * (a[1] - a[0]))
        o[3] = (H * (b[1] - b[0]), -H * (b[0] + b[1]))
    o[2] = rot(o[2], sign)
    return [cadd(e[i], o[i]) for i in range(4)] + [csub(e[i], o[i]) for i in range(4)]


def dft32(load, store, sign):
    mid = {}
    for n2 in range(4):
        out = dft8([load(4 * n1 + n2) for n1 in range(8)], sign)
        for k1 in range(8):
            v = out[k1]
            if n2 * k1 == 4:
                v = (H * (v[0] - sign * v[1]), H * (v[1] + sign * v[0]))
            elif n2 * k1:
                turn = sign * 2.0 * math.pi * n2 * k1 / 32
                c, s = math.cos(turn), math.sin(turn)
                v = (v[0] * c - v[1] * s, v[0] * s + v[1] * c)
            mid[n2, k1] = v
    for k1 in range(8):
        out = dft4([mid[n2, k1] for n2 in range(4)], sign)
        for k2 in range(4):
            store(k1 + 8 * k2, out[k2])


def split(x):
    hi = x.astype(BF)
    return hi, (x - hi.astype(F32)).astype(BF)


def dot(a, b):
    return jnp.dot(a, b, preferred_element_type=F32)


def forward_slabs(active, targ, phi, fz, tw, z, s, apart=False):
    count = len(active)

    def pick(u, values):
        total, chosen, row = values[0], 1, list(values)
        for order in range(1, count):
            row = [after - before for before, after in zip(row, row[1:])]
            chosen = chosen * (u - order + 1)
            total = total + row[0] * (chosen // math.factorial(order))
        return total

    def transform(u, n, slab):
        def load(y):
            at = slice(128 * y, 128 * (y + 1))
            t = targ[n, slab, :, at]
            return t * phi[0, slab, :, at], t * phi[1, slab, :, at]

        def store(k, v):
            c, w = tw[k, 0], tw[k, 1]
            s[u, k, :, 0:128] = v[0] * c + v[1] * w
            s[u, k, :, 128:256] = v[1] * c - v[0] * w

        dft32(load, store, -1)

    def multiply(first, last):
        hi, lo = split(s[first:last].reshape((last - first) * 256, 256))
        res = dot(jnp.concatenate([hi, lo, hi], 1), fz[...])
        for u, (n, slab) in enumerate(active[first:last]):
            part = res[256 * u : 256 * (u + 1)]
            base = pl.multiple_of(8 * slab, 8)
            z[n, :, pl.ds(base, 8), :] = part[:, :128].reshape(32, 8, 128)
            z[n, :, pl.ds(64 + base, 8), :] = part[:, 128:].reshape(32, 8, 128)

    if apart:
        for u, (n, slab) in enumerate(active):
            transform(u, n, slab)
            if u % 2 or u == count - 1:
                multiply(u - u % 2, u + 1)
    else:

        @pl.loop(0, count)
        def _(u):
            transform(u, pick(u, [n for n, _ in active]), pick(u, [slab for _, slab in active]))

        multiply(0, count)


def middle(n, kern, fx, ix, z):
    @pl.loop(0, 32 // YA)
    def _(step):
        ks = [step * YA + i for i in range(YA)]
        hi, lo = split(jnp.concatenate([z[n, k] for k in ks], 1))
        res = dot(fx[...], jnp.concatenate([hi, lo, hi], 0))
        kv = jnp.concatenate([kern[k] for k in ks], 1)
        hi, lo = split(res * jnp.concatenate([kv, kv], 0))
        res = dot(ix[...], jnp.concatenate([hi, lo, hi], 0))
        for i in range(YA):
            z[n, step * YA + i] = res[:, 128 * i : 128 * (i + 1)]


def inverse_slabs(n, parity, phi, iz, tw, z, s, part):
    rows = []
    for zz in range(4):
        base = pl.multiple_of(16 * zz + 8 * parity, 8)
        re = z[n, :, pl.ds(base, 8), :].reshape(256, 128)
        im = z[n, :, pl.ds(64 + base, 8), :].reshape(256, 128)
        rows.append(jnp.concatenate([re, im], 1))
    hi, lo = split(jnp.concatenate(rows, 0))
    res = dot(jnp.concatenate([hi, lo, hi], 1), iz[...]).reshape(4, 32, 8, 256)
    for zz in range(4):
        slab = 2 * zz + parity

        def load(k):
            c, w = tw[k, 0], tw[k, 1]
            r, i = res[zz, k, :, 0:128], res[zz, k, :, 128:256]
            return r * c - i * w, i * c + r * w

        def store(y, v):
            at = slice(128 * y, 128 * (y + 1))
            part[zz, :, at] = v[0] * phi[0, slab, :, at] + v[1] * phi[1, slab, :, at]

        dft32(load, store, 1)


def unpack_kernel(kp, kern):
    low = lax.broadcasted_iota(jnp.int32, (64, 128), 1) < 64

    @pl.loop(0, 4)
    def _(slab):
        @pl.loop(0, 4)
        def _(r):
            a, b = kp[slab, r], kp[slab + 4, r]
            kern[slab * 8 + r] = jnp.where(low, a, pltpu.roll(b, 64, 1))
            kern[slab * 8 + 4 + r] = jnp.where(low, pltpu.roll(a, 64, 1), b)


def body(
    orb, kernel, fx_in, ix_in, fz_in, iz_in, tw_in, out,
    phi, targ, kslab, kpk, kp, kern, z, s, part, rcore, acc, extra, fx, ix, fz, iz, tw, send, recv, local,
):
    b = lax.axis_index("band")
    q = lax.axis_index("grid")

    def mod(value, n):
        return lax.rem(value, jnp.int32(n))

    def div(value, n):
        return lax.div(value, jnp.int32(n))

    core, block, x = mod(b, 2), div(b, 2), div(b, 4)
    plane, ylo = div(q, 2), mod(q, 2)
    odd = mod(ylo + block, 2)
    home = mod(core + block, 2)
    chip = block * 2 + odd
    sibling = (block * 2 + 1 - core, q)
    near = (b, plane * 2 + 1 - ylo)
    mine = core == odd
    owner = core == div(plane, 2)
    planes = [plane] + [mod(plane + d, 4) for d in (1, 2, 3)]
    parities = [ylo, 1 - ylo]
    slabs = [[2 * zz + p for p in parities] for zz in planes]
    targets_here = [div(zz, 2) == core for zz in planes]
    kt = mod(plane, 2)
    other = 1 - kt
    band_of = [kt, other, kt, other]
    across = [(b, 2 * zz + ylo) for zz in planes]
    near_slabs = [[2 * zz + mod(ylo + 1 - odd + i, 2) for i in range(2)] for zz in planes]

    def device(h, c, zz):
        h = mod(h + 16, 16)
        half = div(h, 2)
        return (half * 2 + c, zz * 2 + mod(h + half, 2))

    def at_plane(d):
        return across[d]

    def result_device(n, zz):
        return (mod(chip + n, 16), zz * 2 + home)

    count = [0]

    def slots(n):
        count[0] += n
        return count[0] - n

    def remote(src, dst, s, where, r=None):
        return pltpu.make_async_remote_copy(
            src_ref=src, dst_ref=dst, send_sem=send.at[s], recv_sem=recv.at[s if r is None else r],
            device_id=where, device_id_type=MESH,
        )

    sent, sent_owner = [], []

    def start(cp):
        cp.start()
        sent.append(cp)

    loads = [
        pltpu.make_async_copy(src, dst, local.at[i])
        for i, (src, dst) in enumerate(
            [(kernel, kslab), (fx_in, fx), (ix_in, ix), (fz_in, fz), (iz_in, iz), (tw_in, tw)]
        )
    ]
    for cp in loads:
        cp.start()

    barrier = pltpu.get_barrier_semaphore()
    greeted = []
    for dc in range(2):
        for dq in range(8):
            if dc or dq:
                greeted.append((mod(b + dc, 2) + block * 2, mod(q + dq, 8)))
    for dh in (-2, -1, 1, 2):
        greeted.append(device(chip + dh, core, plane))
    for n in (1, 2):
        behind = mod(b - n + 16, 16)
        behind_core = mod(ylo + div(behind, 2), 2)
        for zz in range(4):
            greeted.append(result_device(n, zz))
            greeted.append(device(behind, behind_core, zz))
    for dx in (4, 8, 12):
        greeted.append((mod(b + dx, 16), q))
    for where in greeted:
        pl.semaphore_signal(barrier, inc=1, device_id=where, device_id_type=MESH)
    pl.semaphore_wait(barrier, len(greeted))

    s_first = slots(4)
    firsts = {}
    for k in range(2):
        for dc in range(2):
            c = (core, 1 - core)[dc]
            src, dst = orb.at[2 * c + k], phi.at[k, q]
            firsts[dc, k] = remote(src, dst, s_first + 2 * dc + k, (block * 2 + c, plane * 2 + home), s_first + 2 * ylo + k)
    s_direct = slots(6)

    def direct(d):
        k = planes[d]
        slot = s_direct + 2 * d - 2
        return remote(orb.at[k], phi.at[band_of[d], q], slot, (block * 2 + div(k, 2), k * 2 + home), slot + ylo)

    def direct_wait(d, i):
        piece = phi.at[kt, slabs[d][i]]
        remote(piece, piece, s_direct, (b, q), s_direct + 2 * (4 - d) - 2 + parities[i]).wait_recv()

    for d in (1, 3, 2):
        start(direct(d))
    keeps = [pltpu.make_async_copy(orb.at[2 * core + k], phi.at[k, q], local.at[6 + k]) for k in range(2)]
    for k in range(2):

        @pl.when(mine)
        def _():
            keeps[k].start()

        @pl.when(jnp.logical_not(mine))
        def _():
            firsts[0, k].start()

        start(firsts[1, k])

    def wait_first(i):
        p = parities[i]
        for k in range(2):
            piece = phi.at[k, slabs[0][i]]
            cp = remote(piece, piece, s_first, (b, q), s_first + 2 * p + k)
            if i == 0:

                @pl.when(mine)
                def _():
                    keeps[k].wait()

                @pl.when(jnp.logical_not(mine))
                def _():
                    cp.wait_recv()
            else:
                cp.wait_recv()

    s_step = slots(8)
    s_pass = slots(4)

    def slab_at(d, i):
        return slabs[d][i]

    def step_copy(i, side, k):
        d = (1, 3)[side]
        piece = phi.at[k, slab_at(0, i)]
        return remote(piece, piece, s_step + 4 * i + 2 * side + k, at_plane(d))

    def start_it(cp):
        cp.start()

    def wait_sent(cp):
        cp.wait_send()

    def step_wait(i, side, k):
        piece = phi.at[k, slab_at((3, 1)[side], i)]
        remote(piece, piece, s_step, (b, q), s_step + 4 * i + 2 * side + k).wait_recv()

    def pass_copy(i, which):
        side = (i + which) % 2
        piece = phi.at[band_of[which], slab_at((3, 1)[side], i)]
        return remote(piece, piece, s_pass + 2 * i + which, at_plane((1, 3)[side]), s_pass + 2 * i + band_of[which])

    def pass_wait(i, k):
        piece = phi.at[k, slab_at(2, i)]
        remote(piece, piece, s_pass, (b, q), s_pass + 2 * i + k).wait_recv()

    def unless(condition):
        return pl.when(jnp.logical_not(condition))

    def each_other(i, act):
        for side, d in enumerate((1, 3)):
            act(step_copy(i, side, kt))

            @unless(targets_here[d])
            def _():
                act(step_copy(i, side, other))

    def each_pass(i, act):
        act(pass_copy(i, 0))

        @unless(targets_here[(3, 1)[i]])
        def _():
            act(pass_copy(i, 1))

    s_t0 = slots(8)
    s_t1 = slots(8)
    s_t2 = slots(8)
    s_t1_give = slots(8)
    s_t2_give = slots(8)
    order = [(0, 0), (3, 0), (1, 0), (0, 1), (2, 0), (1, 1), (3, 1), (2, 1)]
    far_back = device(chip - 2, core, plane)
    near_back = device(chip - 1, core, plane)

    def target_slab(n, j):
        d, i = order[j]
        return (slabs[d][i], near_slabs[d][i], slabs[d][1 - i])[n]

    def own_target(j):
        s = target_slab(0, j)
        src = phi.at[kt, s]
        keep = pltpu.make_async_copy(src, targ.at[0, s], local.at[8 + j])
        give = remote(src, targ.at[0, s], s_t0 + j, sibling)
        back = remote(src, targ.at[2, s], s_t2 + j, far_back)
        beside = remote(src, targ.at[1, s], s_t1 + j, near_back)
        return keep, give, back, beside

    def target_ready(j):
        @pl.when(owner)
        def _():
            keep, give, back, beside = own_target(j)
            back.start()
            if j in RELAYED:

                @pl.when(odd == 1)
                def _():
                    beside.start()
            else:
                beside.start()
            give.start()
            keep.start()

    def far_target(j):
        s = target_slab(2, j)
        piece = targ.at[2, s]
        arrive = remote(piece, piece, s_t2, (b, q), s_t2 + j)
        relay = remote(piece, targ.at[1, s], s_t1 + j, near)
        give = remote(piece, piece, s_t2_give + j, sibling)
        return arrive, relay, give

    def far_ready(j):
        @pl.when(owner)
        def _():
            arrive, relay, give = far_target(j)
            arrive.wait_recv()
            if j in RELAYED:

                @pl.when(odd == 0)
                def _():
                    relay.start()

            give.start()

    def near_target(j):
        piece = targ.at[1, target_slab(1, j)]
        return remote(piece, piece, s_t1, (b, q), s_t1 + j), remote(piece, piece, s_t1_give + j, sibling)

    def near_ready(j):
        @pl.when(owner)
        def _():
            arrive, give = near_target(j)
            arrive.wait_recv()
            give.start()

    def wait_target(n, j):
        base = (s_t0, s_t1_give, s_t2_give)[n]

        @pl.when(jnp.logical_not(owner))
        def _():
            piece = targ.at[n, target_slab(n, j)]
            remote(piece, piece, base, (b, q), base + j).wait_recv()

        if n == 0:

            @pl.when(owner)
            def _():
                own_target(j)[0].wait()

    s_kernel = slots(11)
    kx_half = pl.ds(pl.multiple_of(32 * core, 32), 32)
    kernel_first = [
        remote(kpk.at[x, kx_half], kp.at[q, x, kx_half], s_kernel + d - 1, (b, mod(q + d, 8))) for d in range(1, 8)
    ]
    kernel_second = [
        remote(kp.at[:, x, kx_half], kp.at[:, x, kx_half], s_kernel + 6 + d, (mod(b + 4 * d, 16), q)) for d in (1, 3, 2)
    ]
    kernel_third = remote(kp.at[:, :, kx_half], kp.at[:, :, kx_half], s_kernel + 10, sibling)

    def pack_kernel():
        for r in range(4):
            kpk[r] = jnp.concatenate([kslab[:, r, :], kslab[:, r + 4, :]], 1)
        for cp in kernel_first:
            start(cp)
        kp[q, x, kx_half] = kpk[x, kx_half]

    def forward(*active, apart=False):
        for n, j in active:
            wait_target(n, j)
        forward_slabs([(n, target_slab(n, j)) for n, j in active], targ, phi, fz, tw, z, s, apart)

    def near_others(i, side):
        step_wait(i, side, other)

        @unless(owner)
        def _():
            step_wait(i, side, kt)

    def far_others(i):
        pass_wait(i, other)

        @unless(owner)
        def _():
            pass_wait(i, kt)

    def target_here(j):
        @pl.when(owner)
        def _():
            direct_wait(*order[j])

        target_ready(j)

    wait_first(0)
    target_ready(0)
    each_other(0, start_it)
    target_here(1)
    target_here(2)
    loads[0].wait()
    pack_kernel()
    target_here(4)
    target_here(5)
    target_here(6)
    for cp in loads[1:]:
        cp.wait()
    forward((0, 0))
    near_others(0, 0)
    near_others(0, 1)
    each_pass(0, start_it)
    target_here(7)
    wait_first(1)
    target_ready(3)
    each_other(1, start_it)
    far_ready(0)
    forward((0, 1), (0, 2))
    for j in (1, 2, 5, 6, 4):
        far_ready(j)
    forward((0, 3))
    for cp in kernel_first:
        cp.wait_recv()
    for cp in kernel_second:
        start(cp)
    far_ready(7)
    near_others(1, 1)
    near_others(1, 0)
    each_pass(1, start_it)
    far_ready(3)
    far_others(0)
    forward((0, 4), (2, 5), (2, 6), (2, 3))
    for cp in kernel_second:
        cp.wait_recv()
    start(kernel_third)
    forward((0, 5), (0, 6), (2, 7))
    kernel_third.wait_recv()
    unpack_kernel(kp, kern)
    far_others(1)
    forward((0, 7))

    s_core = slots(3)
    s_result = slots(12)

    def core_sum(n):
        return remote(part.at[n, 0], rcore.at[n], s_core + n, sibling)

    def result(n, d):
        zz = planes[d]
        return remote(part.at[n, 1, zz], acc.at[n, plane], s_result + 4 * n + d, result_device(n, zz))

    s_extra = slots(4)
    adds = jnp.logical_and(odd == 0, core == 1)
    gives = jnp.logical_and(odd == 1, core == 1)
    has_near = jnp.logical_or(odd == 1, core == 1)

    def exchange(d):
        return remote(part.at[1, 1, planes[d]], extra.at[planes[d]], s_extra + d, near)

    result_keep = pltpu.make_async_copy(part.at[0, 1, plane], acc.at[0, plane], local.at[16])

    def finish(n):
        core_sum(n).wait_recv()

        @pl.loop(0, 4)
        def _(i):
            part[n, 1, i] = part[n, 1, i] + rcore[n, i]

        held = jnp.logical_or(jnp.logical_and(adds, n == 2), jnp.logical_and(gives, n == 1))

        @unless(held)
        def _():
            for d in (2, 1, 3):
                result(n, d).start()

        @unless(jnp.logical_or(held, jnp.logical_and(n == 0, mine)))
        def _():
            result(n, 0).start()

        @pl.when(jnp.logical_and(gives, n == 1))
        def _():
            for d in (2, 1, 3, 0):
                exchange(d).start()

    @pl.loop(0, 3)
    def _(u):
        n = mod(2 * u, 3)

        @pl.when(u == 1)
        def _():
            for j in range(8):
                near_ready(j)
            forward((2, 0), (2, 1), (2, 2), (2, 4), apart=True)

        @pl.when(u == 2)
        def _():
            for j in (0, 4):
                forward((1, j), (1, j + 1), (1, j + 2), (1, j + 3), apart=True)

        middle(n, kern, fx, ix, z)

        last = div(u, 2)

        @pl.loop(0, 2)
        def _(g):
            place = mod(g + core * last, 2)
            inverse_slabs(n, mod(home + 1 + g + core * last, 2), phi, iz, tw, z, s, part.at[n, place])

            @pl.when(place == 0)
            def _():
                core_sum(n).start()

            @pl.when(place == 1)
            def _():
                finish(n)

    @pl.when(adds)
    def _():
        for d in (2, 1, 3, 0):
            exchange(d).wait_recv()
            part[2, 1, planes[d]] = part[2, 1, planes[d]] + extra[planes[d]]
            result(2, d).start()

    @pl.when(mine)
    def _():
        result_keep.start()
        result_keep.wait()

    for cp in sent:
        cp.wait_send()
    for i in range(2):
        each_other(i, wait_sent)
        each_pass(i, wait_sent)

    @pl.when(jnp.logical_not(mine))
    def _():
        for k in range(2):
            firsts[0, k].wait_send()

    @pl.when(owner)
    def _():
        for j in range(8):
            keep, give, back, beside = own_target(j)
            give.wait_send()
            back.wait_send()
            arrive, relay, pass_on = far_target(j)
            pass_on.wait_send()
            if j in RELAYED:

                @pl.when(odd == 1)
                def _():
                    beside.wait_send()

                @pl.when(odd == 0)
                def _():
                    relay.wait_send()
            else:
                beside.wait_send()
            near_target(j)[1].wait_send()

    for n in range(3):
        core_sum(n).wait_send()
    for d in range(4):
        result(2, d).wait()
        if d:
            result(0, d).wait()

    @unless(mine)
    def _():
        result(0, 0).wait()

    @pl.when(gives)
    def _():
        for d in range(4):
            exchange(d).wait_send()

    @unless(gives)
    def _():
        for d in range(4):
            result(1, d).wait_send()

    @pl.when(has_near)
    def _():
        for d in range(4):
            result(1, d).wait_recv()

        @pl.loop(0, 4)
        def _(i):
            out[i] = acc[0, i] + acc[1, i] + acc[2, i]

    @unless(has_near)
    def _():
        @pl.loop(0, 4)
        def _(i):
            out[i] = acc[0, i] + acc[2, i]


def local(orbitals, kernel):
    vmem = pl.BlockSpec(memory_space=pltpu.VMEM)
    anywhere = pl.BlockSpec(memory_space=pl.ANY)
    constants = [jnp.asarray(table) for table in tables()]
    return pl.pallas_call(
        body,
        out_shape=pltpu.VMEM(orbitals.shape, F32),
        in_specs=[anywhere] * 7,
        out_specs=vmem,
        scratch_shapes=[
            pltpu.VMEM((2, 8, 8, 4096), F32),
            pltpu.VMEM((3, 8, 8, 4096), F32),
            pltpu.VMEM((64, 8, 64), F32),
            pltpu.VMEM((4, 64, 128), F32),
            pltpu.VMEM((8, 4, 64, 128), F32),
            pltpu.VMEM((32, 64, 128), F32),
            pltpu.VMEM((3, 32, 128, 128), F32),
            pltpu.VMEM((5, 32, 8, 256), F32),
            pltpu.VMEM((3, 2, 4, 8, 4096), F32),
            pltpu.VMEM((3, 4, 8, 4096), F32),
            pltpu.VMEM((3, 4, 8, 4096), F32),
            pltpu.VMEM((4, 8, 4096), F32),
        ]
        + [pltpu.VMEM(table.shape, table.dtype) for table in constants]
        + [
            pltpu.SemaphoreType.DMA((92,)),
            pltpu.SemaphoreType.DMA((92,)),
            pltpu.SemaphoreType.DMA((17,)),
        ],
        compiler_params=pltpu.CompilerParams(
            collective_id=0, has_side_effects=True, vmem_limit_bytes=56 * 2**20
        ),
    )(orbitals, kernel, *constants)


def solution(mesh):
    return jax.shard_map(
        local,
        mesh=mesh,
        in_specs=(P("band", "grid", None), P(None, "grid", None)),
        out_specs=P("band", "grid", None),
        check_vma=False,
    )
```
